128 devices in a mesh: freq: 4 (over x_lo, core), chan: 32 (over x_hi, z, y).
Axes of the slice: x: 4 (x_hi: 2, x_lo: 2; x = x_hi * 2 + x_lo), y: 4, z: 4, core: 2. Of those that a mesh axis runs over, the one named last changes fastest.
Arguments:
- records: float32 [2048, 32768], P(('freq', 'chan')), may hold values from -6 to 6
- sources: int32 [128], replicated, may hold values from 0 to 2047
- dead_list: int32 [32], replicated, may hold values from 0 to 2047
Outputs:
- correlation: float32 [128, 256, 2048], P('chan', 'freq')
The draws below stay inside these ranges and needn't reach their ends.
Inputs may be any that keep to these rules, and one draw needn't show every extreme that they name: Slots 4 b to 4 (b + 1) - 1 are the sources whose correlations chan position b holds; their channels may be any channel of the array and may repeat. `dead_list`: a channel may repeat.
All inputs are finite; a program needn't handle non-finite values.
Results may differ from the reference program's by a relative error of at most 0.004.
Values may be sent and summed in bfloat16 or wider, within the bound.
No kernel may reach another device: no remote copies, remote signals or barrier semaphores. Data moves between devices by JAX's collectives and lax.ppermute only.
A program may use at most 128 MiB of HBM per device.

```python
import jax
import jax.numpy as jnp
from jax import lax

CHANNELS = 2048
NT = 1024
LAGS = 256
DEAD = 32
SEG = 8
NBINS = 512
NSRC = 128
SAMPLES = 32768
N_FREQ = 4


def plant(values, rng, smallest, largest):
    longest = values.shape.index(max(values.shape))
    spots = []
    for shift in (0, 1):
        where = [jax.random.randint(jax.random.fold_in(rng, axis), (), 0, length) for axis, length in enumerate(values.shape)]
        where[longest] = (where[longest] + shift) % values.shape[longest]
        spots.append(tuple(where))
    return values.at[spots[0]].set(smallest).at[spots[1]].set(largest)


def level_of(stream_key, extent, split, smallest, high):
    level, own = 1.0, jax.random.fold_in(stream_key, 6)
    for position, parts in split:
        steps = jnp.exp(jax.random.uniform(jax.random.fold_in(own, position), (parts,), jnp.float32, smallest / len(split), high / len(split)))
        level = level * jnp.repeat(steps, extent[position] // parts).reshape([-1 if axis == position else 1 for axis in range(len(extent))])
    return level


def scatter_about(key, dims, spread, reach, shards=(), held_as=jnp.bfloat16):
    result = spread * jax.random.normal(key, dims, jnp.float32)
    if shards:
        result = result * level_of(key, dims, shards, -0.22, 0.18)
    return jnp.clip(result, -reach, reach).astype(held_as)


def setup_inputs(seed: int = 0) -> dict:
    streams_of = jax.random.split(jax.random.key(seed), 4)
    records = scatter_about(streams_of[0], (CHANNELS, SAMPLES), 1.0, 6.0, ((0, 128),), jnp.float32)
    sources = plant(jax.random.randint(streams_of[1], (NSRC,), 0, CHANNELS), jax.random.fold_in(streams_of[1], 1), 0, CHANNELS - 1).astype(jnp.int32)
    dead_list = plant(jax.random.randint(streams_of[2], (DEAD,), 0, CHANNELS), jax.random.fold_in(streams_of[2], 1), 0, CHANNELS - 1).astype(jnp.int32)
    return {"records": records, "sources": sources, "dead_list": dead_list}


def fir_matrix():
    row_index = jnp.arange(768).astype(jnp.int32)[:, None]
    col_index = jnp.arange(128).astype(jnp.int32)[None, :]
    offset = 4 * col_index + 255 - row_index
    inside = (offset >= 0) & (offset <= 254)
    tap_pos = offset.astype(jnp.float32)
    hamming = 0.54 - 0.46 * jnp.cos(2.0 * jnp.pi * tap_pos / 254.0)
    values = 0.2 * jnp.sinc(0.2 * (tap_pos - 127.0)) * hamming
    return jnp.where(inside, values, 0.0).astype(jnp.float32)

def decimate(records):
    channels, samples = records.shape
    blocks = samples // 512
    padded = jnp.pad(records, ((0, 0), (128, 384))).reshape(channels, blocks + 1, 512)
    windows = jnp.concatenate([padded[:, :blocks], padded[:, 1:, :256]], axis=2).reshape(channels * blocks, 768)
    filtered = jnp.dot(windows, fir_matrix(), precision=lax.Precision.HIGHEST, preferred_element_type=jnp.float32)
    return filtered.reshape(channels, blocks * 128)

def dft_table(quarters, shard_bins):
    sample_index = jnp.arange(NT).astype(jnp.int32)
    column = jnp.arange(NT).astype(jnp.int32)
    quarter = column // (2 * shard_bins)
    part_index = column // shard_bins % 2
    bin_index = 1 + quarter * shard_bins + column % shard_bins
    phase_index = sample_index[:, None] * bin_index[None, :] % NT
    angle = phase_index.astype(jnp.float32) * (2.0 * jnp.pi / NT)
    return jnp.where(part_index[None, :] == 0, jnp.cos(angle), -jnp.sin(angle)).astype(jnp.float32)

def whiten(records, alive_mask, quarters):
    shard_bins = NBINS // quarters
    channels = records.shape[0]
    decimated = decimate(records)
    segments = decimated.reshape(channels * SEG, NT)
    spectra = jnp.dot(segments, dft_table(quarters, shard_bins), precision=lax.Precision.HIGHEST, preferred_element_type=jnp.float32)
    spectrum_parts = spectra.reshape(-1, quarters, 2, shard_bins)
    real_part = spectrum_parts[:, :, 0, :]
    imag_part = spectrum_parts[:, :, 1, :]
    power_bins = (real_part * real_part + imag_part * imag_part).reshape(-1, NBINS)
    bin_range = jnp.arange(NBINS).astype(jnp.int32)
    smoother = (jnp.abs(bin_range[:, None] - bin_range[None, :]) <= 32).astype(jnp.float32)
    level = jnp.dot(power_bins, smoother, precision=lax.Precision.HIGHEST, preferred_element_type=jnp.float32) / 65.0
    inverse_level = lax.rsqrt(level + 1e-06).reshape(-1, quarters, 1, shard_bins)
    whitened = (spectrum_parts * inverse_level).reshape(channels, SEG, NT) * alive_mask[:, None, None]
    return whitened.astype(jnp.bfloat16)

def lag_tables(quarter, shard_bins):
    bin_index = 1 + quarter * shard_bins + jnp.arange(shard_bins).astype(jnp.int32)
    lag_values = jnp.arange(LAGS).astype(jnp.int32) - LAGS // 2
    phase_index = bin_index[:, None] * (lag_values % NT)[None, :] % NT
    angle = phase_index.astype(jnp.float32) * (2.0 * jnp.pi / NT)
    return (jnp.cos(angle), jnp.sin(angle))

def lagged_rows(spectrum_parts, cosine_table, sine_table, lag_scale):
    real_part = spectrum_parts[:, None, :, 0, :]
    imag_part = spectrum_parts[:, None, :, 1, :]
    cos_rows = cosine_table.T[None, :, None, :]
    sin_rows = sine_table.T[None, :, None, :]
    rotated_re = real_part * cos_rows - imag_part * sin_rows
    rotated_im = real_part * sin_rows + imag_part * cos_rows
    stacked = jnp.stack([rotated_re, rotated_im], axis=3) * lag_scale
    return stacked.reshape(stacked.shape[0] * stacked.shape[1], -1).astype(jnp.bfloat16)

def reference(records, sources, dead_list):
    channel_ids = jnp.arange(CHANNELS).astype(jnp.int32)
    alive_mask = jnp.all(dead_list[None, :] != channel_ids[:, None], axis=1).astype(jnp.float32)
    whitened = whiten(records, alive_mask, N_FREQ)
    shard_bins = NBINS // N_FREQ
    row_width = SEG * 2 * shard_bins
    blocks = whitened.reshape(CHANNELS, SEG, N_FREQ, 2 * shard_bins)
    quarter_data = [blocks[:, :, quarter].reshape(CHANNELS, row_width) for quarter in range(N_FREQ)]
    quarter_tables = [lag_tables(quarter, shard_bins) for quarter in range(N_FREQ)]
    lag_scale = 1.0 / jnp.sqrt(jnp.float32(SEG * NBINS))
    picked = whitened[sources]

    def one_source(source_row):
        spectrum_parts = source_row.astype(jnp.float32).reshape(SEG, N_FREQ, 2, shard_bins)
        running = jnp.zeros((LAGS, CHANNELS), jnp.float32)
        for quarter in range(N_FREQ):
            cosine_table, sine_table = quarter_tables[quarter]
            lagged = lagged_rows(spectrum_parts[None, :, quarter], cosine_table, sine_table, lag_scale)
            running = running + lax.dot_general(lagged, quarter_data[quarter], (((1,), (1,)), ((), ())), preferred_element_type=jnp.float32)
        return running
    return lax.map(one_source, picked)
```

```python
import numpy as np
import jax
import jax.numpy as jnp
from jax import lax
from jax.experimental import pallas as pl
from jax.experimental.pallas import tpu as pltpu
from jax.sharding import Mesh, PartitionSpec as P

NT = 1024
LAGS = 256
SEG = 8
NBINS = 512
OWN = 16
GROUP = 4
PLANE = 32
LINE = GROUP * OWN
AXES = ("f", "xh", "z", "y")
PLANE_AXES = ("f", "xh", "z")
HIGHEST = lax.Precision.HIGHEST
F32 = jnp.float32
BF16 = jnp.bfloat16


def fir_table():
    row = np.arange(768)[:, None]
    col = np.arange(128)[None, :]
    offset = 4 * col + 255 - row
    inside = (offset >= 0) & (offset <= 254)
    tap = offset.astype(np.float64)
    hamming = 0.54 - 0.46 * np.cos(2.0 * np.pi * tap / 254.0)
    values = 0.2 * np.sinc(0.2 * (tap - 127.0)) * hamming
    return np.where(inside, values, 0.0).astype(np.float32)


def dft_table():
    sample = np.arange(NT)[:, None]
    bins = 1 + np.arange(NBINS)[None, :]
    angle = (sample * bins % NT) * (2.0 * np.pi / NT)
    return np.concatenate([np.cos(angle), -np.sin(angle)], axis=1).astype(np.float32)


def smooth_table():
    bins = np.arange(NBINS)
    return (np.abs(bins[:, None] - bins[None, :]) <= 32).astype(np.float32)


def lag_table():
    bins = 1 + np.arange(NBINS)[None, :]
    lags = (np.arange(LAGS) - LAGS // 2)[:, None]
    angle = (bins * lags % NT) * (2.0 * np.pi / NT)
    table = np.concatenate([np.cos(angle), -np.sin(angle)], axis=1)
    return table / np.sqrt(SEG * NBINS)


def whiten_kernel(base_ref, x_ref, fir_ref, dft_ref, smooth_ref, dead_ref, out_ref, win_ref, seg_ref):
    for block in range(64):
        rows = pl.ds(block * OWN, OWN)
        start = block * 512 - 128
        if block == 0:
            win_ref[rows, 0:128] = jnp.zeros((OWN, 128), F32)
            win_ref[rows, 128:768] = x_ref[:, 0:640]
        elif block == 63:
            win_ref[rows, 0:640] = x_ref[:, start : start + 640]
            win_ref[rows, 640:768] = jnp.zeros((OWN, 128), F32)
        else:
            win_ref[rows, :] = x_ref[:, start : start + 768]
    decimated = jnp.dot(win_ref[...], fir_ref[...], precision=HIGHEST, preferred_element_type=F32)
    for block in range(64):
        segment, part = block // 8, block % 8
        seg_ref[segment * OWN : (segment + 1) * OWN, part * 128 : (part + 1) * 128] = decimated[
            block * OWN : (block + 1) * OWN
        ]
    spectra = jnp.dot(seg_ref[...], dft_ref[...], precision=HIGHEST, preferred_element_type=F32)
    real_part = spectra[:, :NBINS]
    imag_part = spectra[:, NBINS:]
    power = real_part * real_part + imag_part * imag_part
    level = jnp.dot(power, smooth_ref[...], precision=HIGHEST, preferred_element_type=F32) / 65.0
    own_ids = base_ref[0] + (lax.broadcasted_iota(jnp.int32, (SEG * OWN, 32), 0) & (OWN - 1))
    dead = jnp.max(jnp.where(dead_ref[...] == own_ids, 1.0, 0.0), axis=1, keepdims=True)
    scale = lax.rsqrt(level + 1e-06) * (1.0 - dead)
    real_part = (real_part * scale).reshape(SEG, OWN, NBINS).astype(BF16)
    imag_part = (imag_part * scale).reshape(SEG, OWN, NBINS).astype(BF16)
    for copy in range(GROUP):
        out_ref[copy, 0:SEG] = real_part
        out_ref[copy, SEG : 2 * SEG] = imag_part


def pick_kernel(place_ref, sources_ref, line_ref, out_ref, wide_ref):
    wide = line_ref[...].astype(F32).reshape(GROUP * 2 * SEG * OWN, NBINS)
    for col in range(NBINS // 128):
        wide_ref[col] = wide[:, col * 128 : (col + 1) * 128]
    for slot in range(PLANE):
        quarter, block = slot // 8, slot % 8
        index = 4 * ((block // 4) * 16 + (block % 4) * 4 + place_ref[0]) + quarter
        channel = sources_ref[index]
        first = ((channel >> 4) & 3) * (2 * SEG * OWN) + (channel & (OWN - 1))
        for col in range(NBINS // 128):
            rows = wide_ref[col, pl.ds(first, 2 * SEG, stride=OWN), :]
            out_ref[slot, :, col * 128 : (col + 1) * 128] = rows.astype(BF16)


def corr_kernel(source_ref, line_ref, lag_ref, out_ref, chan_ref, src_ref, cross_ref):
    for segment in range(SEG):
        real_part = line_ref[:, segment].reshape(LINE, NBINS).astype(F32)
        imag_part = line_ref[:, SEG + segment].reshape(LINE, NBINS).astype(F32)
        chan_ref[0, segment] = real_part
        chan_ref[1, segment] = real_part - imag_part
        chan_ref[2, segment] = real_part + imag_part
    wide = source_ref[...].astype(F32)
    src_ref[:, 0:SEG] = wide[:, 0:SEG] + wide[:, SEG:]
    src_ref[:, SEG : 2 * SEG] = wide[:, SEG:]
    src_ref[:, 2 * SEG :] = wide[:, 0:SEG]

    def block_step(block, carry):
        def quarter_step(quarter, inner):
            slot = quarter * 8 + block
            for col in range(NBINS // 128):
                lanes = pl.ds(col * 128, 128)
                source_rows = src_ref[slot, :, lanes]
                for tile in range(LINE // 16):
                    rows = pl.ds(tile * 16, 16)
                    sums = []
                    for kind in range(3):
                        total = None
                        for segment in range(SEG):
                            row = kind * SEG + segment
                            term = source_rows[row : row + 1] * chan_ref[kind, segment, rows, lanes]
                            total = term if total is None else total + term
                        sums.append(total)
                    place = pl.ds(pl.multiple_of(quarter * LINE + tile * 16, 16), 16)
                    cross_ref[place, col * 128 : (col + 1) * 128] = (sums[0] - sums[1]).astype(BF16)
                    cross_ref[place, NBINS + col * 128 : NBINS + (col + 1) * 128] = (
                        sums[0] - sums[2]
                    ).astype(BF16)
            return inner

        lax.fori_loop(0, 4, quarter_step, 0)
        result = lax.dot_general(
            lag_ref[...], cross_ref[...], (((1,), (1,)), ((), ())), preferred_element_type=F32
        ).astype(BF16)
        for part in range(4):
            out_ref[part, block] = result[part * 64 : (part + 1) * 64]
        return carry

    lax.fori_loop(0, 8, block_step, 0)


def spread_kernel(in_ref, out_ref):
    for pair in range(4):
        left = in_ref[2 * pair].astype(F32)
        right = in_ref[2 * pair + 1].astype(F32)
        for quarter in range(4):
            lanes = slice(quarter * LINE, (quarter + 1) * LINE)
            out_ref[quarter, :, pair * 128 : (pair + 1) * 128] = jnp.concatenate(
                [left[:, lanes], right[:, lanes]], axis=1
            )


def vmem():
    return pl.BlockSpec(memory_space=pltpu.VMEM)


def smem():
    return pl.BlockSpec(memory_space=pltpu.SMEM)


LIMIT = pltpu.CompilerParams(vmem_limit_bytes=48 * 1024 * 1024)


def shards(records, sources, dead_list):
    f_pos = lax.axis_index("f")
    xh_pos = lax.axis_index("xh")
    z_pos = lax.axis_index("z")
    y_pos = lax.axis_index("y")
    device = ((f_pos * 2 + xh_pos) * 4 + z_pos) * 4 + y_pos
    whitened = pl.pallas_call(
        whiten_kernel,
        out_shape=jax.ShapeDtypeStruct((GROUP, 2 * SEG, OWN, NBINS), BF16),
        in_specs=[smem(), vmem(), vmem(), vmem(), vmem(), vmem()],
        out_specs=vmem(),
        scratch_shapes=[pltpu.VMEM((64 * OWN, 768), F32), pltpu.VMEM((SEG * OWN, NT), F32)],
        compiler_params=LIMIT,
        name="whiten",
    )(
        (device * OWN).reshape(1),
        records,
        jnp.asarray(fir_table()),
        jnp.asarray(dft_table()),
        jnp.asarray(smooth_table()),
        dead_list.reshape(1, 32),
    )
    line = lax.all_to_all(whitened, "y", 0, 0, tiled=True)
    picked = pl.pallas_call(
        pick_kernel,
        out_shape=jax.ShapeDtypeStruct((PLANE, 2 * SEG, NBINS), BF16),
        in_specs=[smem(), smem(), vmem()],
        out_specs=vmem(),
        scratch_shapes=[pltpu.VMEM((NBINS // 128, GROUP * 2 * SEG * OWN, 128), F32)],
        compiler_params=LIMIT,
        name="pick",
    )(y_pos.reshape(1), sources, line)
    arrived = lax.all_to_all(picked, PLANE_AXES, 0, 0, tiled=True)
    channel = sources[4 * (xh_pos * 16 + z_pos * 4 + y_pos) + f_pos]
    held = lax.dynamic_index_in_dim(arrived, channel >> 6, 0, keepdims=True)
    held_all = jnp.broadcast_to(held, (PLANE, 2 * SEG, NBINS))
    source_spectra = lax.all_to_all(held_all, PLANE_AXES, 0, 0, tiled=True)
    blocks = pl.pallas_call(
        corr_kernel,
        out_shape=jax.ShapeDtypeStruct((4, 8, LAGS // 4, 4 * LINE), BF16),
        in_specs=[vmem(), vmem(), vmem()],
        out_specs=vmem(),
        scratch_shapes=[
            pltpu.VMEM((3, SEG, LINE, NBINS), F32),
            pltpu.VMEM((PLANE, 3 * SEG, NBINS), F32),
            pltpu.VMEM((4 * LINE, 2 * NBINS), BF16),
        ],
        compiler_params=LIMIT,
        name="correlate",
    )(source_spectra, line, jnp.asarray(lag_table(), dtype=BF16))
    gathered = lax.all_to_all(
        blocks.reshape(PLANE, LAGS // 4, 4 * LINE), PLANE_AXES, 0, 0, tiled=True
    )
    return pl.pallas_call(
        spread_kernel,
        grid=(4,),
        out_shape=jax.ShapeDtypeStruct((4, LAGS // 4, PLANE * LINE), F32),
        in_specs=[pl.BlockSpec((8, LAGS // 4, 4 * LINE), lambda i: (i, 0, 0))],
        out_specs=pl.BlockSpec((4, LAGS // 4, 8 * LINE), lambda i: (0, 0, i)),
        compiler_params=LIMIT,
        name="spread",
    )(gathered)


def solution(mesh):
    inner = Mesh(mesh.devices.reshape(4, 2, 4, 4), AXES)
    return jax.shard_map(
        shards,
        mesh=inner,
        in_specs=(P(AXES, None), P(), P()),
        out_specs=P(("xh", "z", "y"), "f", None),
        check_vma=False,
    )
```

```python
import numpy as np
import jax
import jax.numpy as jnp
from jax import lax
from jax.experimental import pallas as pl
from jax.experimental.pallas import tpu as pltpu
from jax.sharding import Mesh, PartitionSpec as P

NT = 1024
LAGS = 256
SEG = 8
NBINS = 512
OWN = 16
GROUP = 4
PLANE = 32
LINE = GROUP * OWN
AXES = ("f", "xh", "z", "y")
PLANE_AXES = ("f", "xh", "z")
BIN_ORDER = np.concatenate([np.arange(2, NBINS + 1, 2), np.arange(1, NBINS, 2)])
PIECES = (0, 8320, 16512, 24704, 32768)
F32 = jnp.float32
BF16 = jnp.bfloat16


def split_table(table, terms):
    left = table.astype(np.float64)
    parts = []
    for _ in range(terms):
        part = left.astype(np.float32).astype(BF16)
        parts.append(part)
        left = left - part.astype(np.float64)
    return parts


def fir_table():
    row = np.arange(768)[:, None]
    col = np.arange(128)[None, :]
    offset = 4 * col + 255 - row
    inside = (offset >= 0) & (offset <= 254)
    tap = offset.astype(np.float64)
    hamming = 0.54 - 0.46 * np.cos(2.0 * np.pi * tap / 254.0)
    values = 0.2 * np.sinc(0.2 * (tap - 127.0)) * hamming
    return np.concatenate(split_table(np.where(inside, values, 0.0), 2), axis=1)


def dft_table():
    sample = np.arange(NT // 2)[:, None]
    tables = []
    for bins in (BIN_ORDER[: NBINS // 2], BIN_ORDER[NBINS // 2 :]):
        angle = (sample * bins[None, :] % NT) * (2.0 * np.pi / NT)
        table = np.concatenate([np.cos(angle), -np.sin(angle)], axis=1)
        tables.append(np.stack(split_table(table, 3)))
    return np.stack(tables)


def smooth_table():
    return (np.abs(BIN_ORDER[:, None] - BIN_ORDER[None, :]) <= 32).astype(BF16)


def lag_table():
    lags = (np.arange(LAGS) - LAGS // 2)[:, None]
    angle = (BIN_ORDER[None, :] * lags % NT) * (2.0 * np.pi / NT)
    table = np.concatenate([np.cos(angle), -np.sin(angle)], axis=1)
    return (table / np.sqrt(SEG * NBINS)).astype(np.float32).astype(BF16)


def split_rows(value, terms):
    parts = []
    for term in range(terms):
        part = value.astype(BF16)
        parts.append(part)
        if term < terms - 1:
            value = value - part.astype(F32)
    return parts


def whiten_kernel(
    base_ref, x_hbm, fir_hbm, dft_hbm, smooth_hbm, dead_ref, out_ref,
    x_ref, fir_ref, dft_ref, smooth_ref, seg_ref, turn_ref, sems,
):
    copies = [pltpu.make_async_copy(fir_hbm, fir_ref, sems.at[0])]
    for piece in range(4):
        lanes = pl.ds(PIECES[piece], PIECES[piece + 1] - PIECES[piece])
        copies.append(
            pltpu.make_async_copy(x_hbm.at[:, lanes], x_ref.at[:, lanes], sems.at[1 + piece])
        )
    copies.append(pltpu.make_async_copy(dft_hbm, dft_ref, sems.at[5]))
    copies.append(pltpu.make_async_copy(smooth_hbm, smooth_ref, sems.at[6]))
    for copy in copies:
        copy.start()
    copies[0].wait()
    edge = jnp.zeros((OWN, 128), F32)
    for piece in range(4):
        copies[1 + piece].wait()
        rows = x_ref[:, max(8192 * piece - 128, 0) : min(8192 * piece + 8320, 32768)]
        if piece == 0:
            rows = jnp.concatenate([edge, rows], axis=1)
        if piece == 3:
            rows = jnp.concatenate([rows, edge], axis=1)
        windows = jnp.concatenate(
            [part[:, 512 * b : 512 * b + 768] for part in split_rows(rows, 3) for b in range(16)],
            axis=0,
        )
        product = jnp.dot(windows, fir_ref[...], preferred_element_type=F32)
        decimated = product[0:256, :128] + (
            product[0:256, 128:]
            + (product[256:512, :128] + (product[256:512, 128:] + product[512:768, :128]))
        )
        for b in range(16):
            segment, part = 2 * piece + b // 8, b % 8
            seg_ref[segment * OWN : (segment + 1) * OWN, part * 128 : (part + 1) * 128] = (
                decimated[b * OWN : (b + 1) * OWN]
            )
    copies[5].wait()
    copies[6].wait()
    rows = SEG * OWN
    first, second = seg_ref[:, : NT // 2], seg_ref[:, NT // 2 :]
    halves = []
    for parity, folded in enumerate((first + second, first - second)):
        terms = jnp.concatenate(split_rows(folded, 3), axis=0)
        high = jnp.dot(terms, dft_ref[parity, 0], preferred_element_type=F32)
        mid = jnp.dot(terms[: 2 * rows], dft_ref[parity, 1], preferred_element_type=F32)
        low = jnp.dot(terms[:rows], dft_ref[parity, 2], preferred_element_type=F32)
        halves.append(
            high[:rows] + (high[rows : 2 * rows] + mid[:rows] + (high[2 * rows :] + mid[rows:] + low))
        )
    cut = NBINS // 2
    real_part = jnp.concatenate([halves[0][:, :cut], halves[1][:, :cut]], axis=1)
    imag_part = jnp.concatenate([halves[0][:, cut:], halves[1][:, cut:]], axis=1)
    power = real_part * real_part + imag_part * imag_part
    sums = jnp.dot(
        jnp.concatenate(split_rows(power, 2), axis=0), smooth_ref[...], preferred_element_type=F32
    )
    level = (sums[:rows] + sums[rows:]) / 65.0
    own_ids = base_ref[0] + (lax.broadcasted_iota(jnp.int32, (rows, 32), 0) & (OWN - 1))
    dead = jnp.max(jnp.where(dead_ref[...] == own_ids, 1.0, 0.0), axis=1, keepdims=True)
    scale = lax.rsqrt(level + 1e-06) * (1.0 - dead)
    real_part = real_part * scale
    imag_part = imag_part * scale
    for segment in range(SEG):
        take = slice(segment * OWN, (segment + 1) * OWN)
        for col in range(NBINS // 128):
            lanes = slice(col * 128, (col + 1) * 128)
            turn_ref[col, pl.ds(segment, OWN, stride=2 * SEG), :] = real_part[take, lanes]
            turn_ref[col, pl.ds(SEG + segment, OWN, stride=2 * SEG), :] = imag_part[take, lanes]
    for col in range(NBINS // 128):
        turned = turn_ref[col].reshape(OWN, 2 * SEG, 128).astype(BF16)
        for copy in range(GROUP):
            out_ref[copy, :, :, col * 128 : (col + 1) * 128] = turned


def pick_kernel(place_ref, sources_ref, line_ref, out_ref):
    for slot in range(PLANE):
        quarter, block = slot // 8, slot % 8
        index = 4 * ((block // 4) * 16 + (block % 4) * 4 + place_ref[0]) + quarter
        out_ref[slot] = line_ref[sources_ref[index] & (LINE - 1)]


def hold_kernel(owner_ref, arrived_ref, out_ref):
    held = arrived_ref[owner_ref[0]]
    for slot in range(PLANE):
        out_ref[slot] = held


def ready_kernel(line_ref, chan_ref):
    cols = NBINS // 128
    for col in range(cols):
        wide = line_ref[:, :, col * 128 : (col + 1) * 128].astype(F32)
        real_part, imag_part = wide[:, :SEG], wide[:, SEG:]
        for kind, rows in enumerate((real_part, real_part - imag_part, real_part + imag_part)):
            chan_ref[kind * cols + col] = rows.reshape(LINE * SEG, 128)


def corr_kernel(source_ref, chan_ref, lag_ref, out_ref, src_ref, cross_ref):
    cols = NBINS // 128
    wide = source_ref[...].astype(F32)
    src_ref[:, 0:SEG] = wide[:, 0:SEG] + wide[:, SEG:]
    src_ref[:, SEG : 2 * SEG] = wide[:, SEG:]
    src_ref[:, 2 * SEG :] = wide[:, 0:SEG]

    def block_step(block, carry):
        for col in range(cols):
            lanes = slice(col * 128, (col + 1) * 128)
            for tile in range(LINE // 16):

                def sums(kind):
                    totals = [None] * 4
                    for segment in range(SEG):
                        rows = pl.ds(tile * 16 * SEG + segment, 16, stride=SEG)
                        channel_rows = chan_ref[kind * cols + col, rows, :]
                        for quarter in range(4):
                            row = src_ref[quarter * 8 + block, pl.ds(kind * SEG + segment, 1), lanes]
                            term = row * channel_rows
                            old = totals[quarter]
                            totals[quarter] = term if old is None else old + term
                    return totals

                common = sums(0)
                for kind in (1, 2):
                    other = sums(kind)
                    spot = (kind - 1) * NBINS + col * 128
                    for quarter in range(4):
                        first = block * 4 * LINE + quarter * LINE + tile * 16
                        cross_ref[pl.ds(pl.multiple_of(first, 16), 16), spot : spot + 128] = (
                            common[quarter] - other[quarter]
                        ).astype(BF16)
        return carry

    lax.fori_loop(0, 8, block_step, 0)
    for half in range(2):
        pairs = 16 * LINE
        result = lax.dot_general(
            lag_ref[...],
            cross_ref[half * pairs : (half + 1) * pairs],
            (((1,), (1,)), ((), ())),
            preferred_element_type=F32,
        ).astype(BF16)
        for block in range(4):
            for part in range(4):
                out_ref[part, 4 * half + block] = result[
                    part * 64 : (part + 1) * 64, block * 4 * LINE : (block + 1) * 4 * LINE
                ]


def spread_kernel(in_ref, out_ref):
    for pair in range(4):
        left = in_ref[2 * pair].astype(F32)
        right = in_ref[2 * pair + 1].astype(F32)
        for quarter in range(4):
            lanes = slice(quarter * LINE, (quarter + 1) * LINE)
            out_ref[quarter, :, pair * 128 : (pair + 1) * 128] = jnp.concatenate(
                [left[:, lanes], right[:, lanes]], axis=1
            )


def vmem():
    return pl.BlockSpec(memory_space=pltpu.VMEM)


def smem():
    return pl.BlockSpec(memory_space=pltpu.SMEM)


def whole():
    return pl.BlockSpec(memory_space=pl.ANY)


LIMIT = pltpu.CompilerParams(vmem_limit_bytes=48 * 1024 * 1024)
FULL = pltpu.CompilerParams(vmem_limit_bytes=60 * 1024 * 1024)


def call_whiten(base, records, dead_list):
    return pl.pallas_call(
        whiten_kernel,
        out_shape=jax.ShapeDtypeStruct((GROUP, OWN, 2 * SEG, NBINS), BF16),
        in_specs=[smem(), whole(), whole(), whole(), whole(), vmem()],
        out_specs=vmem(),
        scratch_shapes=[
            pltpu.VMEM((OWN, 32768), F32),
            pltpu.VMEM((768, 256), BF16),
            pltpu.VMEM((2, 3, NT // 2, NBINS), BF16),
            pltpu.VMEM((NBINS, NBINS), BF16),
            pltpu.VMEM((SEG * OWN, NT), F32),
            pltpu.VMEM((NBINS // 128, OWN * 2 * SEG, 128), F32),
            pltpu.SemaphoreType.DMA((7,)),
        ],
        compiler_params=FULL,
        name="whiten",
    )(
        base,
        records,
        jnp.asarray(fir_table()),
        jnp.asarray(dft_table()),
        jnp.asarray(smooth_table()),
        dead_list.reshape(1, 32),
    )


def call_pick(place, sources, line):
    return pl.pallas_call(
        pick_kernel,
        out_shape=jax.ShapeDtypeStruct((PLANE, 2 * SEG, NBINS), BF16),
        in_specs=[smem(), smem(), vmem()],
        out_specs=vmem(),
        compiler_params=LIMIT,
        name="pick",
    )(place, sources, line)


def call_hold(owner, arrived):
    return pl.pallas_call(
        hold_kernel,
        out_shape=jax.ShapeDtypeStruct((PLANE, 2 * SEG, NBINS), BF16),
        in_specs=[smem(), vmem()],
        out_specs=vmem(),
        compiler_params=LIMIT,
        name="hold",
    )(owner, arrived)


def call_ready(line):
    return pl.pallas_call(
        ready_kernel,
        out_shape=jax.ShapeDtypeStruct((3 * (NBINS // 128), LINE * SEG, 128), F32),
        in_specs=[vmem()],
        out_specs=vmem(),
        compiler_params=LIMIT,
        cost_estimate=pl.CostEstimate(flops=1000000, bytes_accessed=4194304, transcendentals=0),
        name="ready",
    )(line)


def call_corr(source_spectra, chan):
    return pl.pallas_call(
        corr_kernel,
        out_shape=jax.ShapeDtypeStruct((4, 8, LAGS // 4, 4 * LINE), BF16),
        in_specs=[vmem(), vmem(), vmem()],
        out_specs=vmem(),
        scratch_shapes=[
            pltpu.VMEM((PLANE, 3 * SEG, NBINS), F32),
            pltpu.VMEM((PLANE * LINE, 2 * NBINS), BF16),
        ],
        compiler_params=LIMIT,
        name="correlate",
    )(source_spectra, chan, jnp.asarray(lag_table()))


def call_spread(gathered):
    return pl.pallas_call(
        spread_kernel,
        grid=(4,),
        out_shape=jax.ShapeDtypeStruct((4, LAGS // 4, PLANE * LINE), F32),
        in_specs=[pl.BlockSpec((8, LAGS // 4, 4 * LINE), lambda i: (i, 0, 0))],
        out_specs=pl.BlockSpec((4, LAGS // 4, 8 * LINE), lambda i: (0, 0, i)),
        compiler_params=LIMIT,
        name="spread",
    )(gathered)


def shards(records, sources, dead_list):
    f_pos = lax.axis_index("f")
    xh_pos = lax.axis_index("xh")
    z_pos = lax.axis_index("z")
    y_pos = lax.axis_index("y")
    device = ((f_pos * 2 + xh_pos) * 4 + z_pos) * 4 + y_pos
    own_slot = sources[4 * (xh_pos * 16 + z_pos * 4 + y_pos) + f_pos]
    whitened = call_whiten((device * OWN).reshape(1), records, dead_list)
    line = lax.all_to_all(whitened, "y", 0, 0, tiled=True).reshape(LINE, 2 * SEG, NBINS)
    picked = call_pick(y_pos.reshape(1), sources, line)
    arrived = lax.all_to_all(picked, PLANE_AXES, 0, 0, tiled=True)
    held = call_hold((own_slot >> 6).reshape(1), arrived)
    source_spectra = lax.all_to_all(held, PLANE_AXES, 0, 0, tiled=True)
    blocks = call_corr(source_spectra, call_ready(line)).reshape(PLANE, LAGS // 4, 4 * LINE)
    return call_spread(lax.all_to_all(blocks, PLANE_AXES, 0, 0, tiled=True))


def solution(mesh):
    inner = Mesh(mesh.devices.reshape(4, 2, 4, 4), AXES)
    return jax.shard_map(
        shards,
        mesh=inner,
        in_specs=(P(AXES, None), P(), P()),
        out_specs=P(("xh", "z", "y"), "f", None),
        check_vma=False,
    )
```

```python
import numpy as np
import jax
import jax.numpy as jnp
from jax import lax
from jax.experimental import pallas as pl
from jax.experimental.pallas import tpu as pltpu
from jax.sharding import Mesh, PartitionSpec as P

NT = 1024
LAGS = 256
SEG = 8
NBINS = 512
OWN = 16
GROUP = 4
PLANE = 32
LINE = GROUP * OWN
AXES = ("xl", "core", "xh", "z", "y")
PLANE_AXES = ("xl", "core", "xh", "z")
SIDE_AXES = ("xl", "xh", "z")
SLOTS = 16
BIN_ORDER = np.concatenate([np.arange(2, NBINS + 1, 2), np.arange(1, NBINS, 2)])
PIECES = (0, 8320, 16512, 24704, 32768)
F32 = jnp.float32
BF16 = jnp.bfloat16


def split_table(table, terms):
    left = table.astype(np.float64)
    parts = []
    for _ in range(terms):
        part = left.astype(np.float32).astype(BF16)
        parts.append(part)
        left = left - part.astype(np.float64)
    return parts


def fir_table():
    row = np.arange(768)[:, None]
    col = np.arange(128)[None, :]
    offset = 4 * col + 255 - row
    inside = (offset >= 0) & (offset <= 254)
    tap = offset.astype(np.float64)
    hamming = 0.54 - 0.46 * np.cos(2.0 * np.pi * tap / 254.0)
    values = 0.2 * np.sinc(0.2 * (tap - 127.0)) * hamming
    return np.concatenate(split_table(np.where(inside, values, 0.0), 2), axis=1)


def dft_table():
    sample = np.arange(NT // 2)[:, None]
    tables = []
    for bins in (BIN_ORDER[: NBINS // 2], BIN_ORDER[NBINS // 2 :]):
        angle = (sample * bins[None, :] % NT) * (2.0 * np.pi / NT)
        table = np.concatenate([np.cos(angle), -np.sin(angle)], axis=1)
        tables.append(np.stack(split_table(table, 3)))
    return np.stack(tables)


def smooth_table():
    return (np.abs(BIN_ORDER[:, None] - BIN_ORDER[None, :]) <= 32).astype(BF16)


def lag_table():
    lags = (np.arange(LAGS) - LAGS // 2)[:, None]
    angle = (BIN_ORDER[None, :] * lags % NT) * (2.0 * np.pi / NT)
    table = np.concatenate([np.cos(angle), -np.sin(angle)], axis=1)
    return (table / np.sqrt(SEG * NBINS)).astype(np.float32).astype(BF16)


def split_rows(value, terms):
    parts = []
    for term in range(terms):
        part = value.astype(BF16)
        parts.append(part)
        if term < terms - 1:
            value = value - part.astype(F32)
    return parts


def whiten_kernel(
    base_ref, x_hbm, fir_hbm, dft_hbm, smooth_hbm, dead_ref, out_ref,
    x_ref, fir_ref, dft_ref, smooth_ref, seg_ref, turn_ref, sems,
):
    copies = [pltpu.make_async_copy(fir_hbm, fir_ref, sems.at[0])]
    for piece in range(4):
        lanes = pl.ds(PIECES[piece], PIECES[piece + 1] - PIECES[piece])
        copies.append(
            pltpu.make_async_copy(x_hbm.at[:, lanes], x_ref.at[:, lanes], sems.at[1 + piece])
        )
    copies.append(pltpu.make_async_copy(dft_hbm, dft_ref, sems.at[5]))
    copies.append(pltpu.make_async_copy(smooth_hbm, smooth_ref, sems.at[6]))
    for copy in copies:
        copy.start()
    copies[0].wait()
    edge = jnp.zeros((OWN, 128), F32)
    for piece in range(4):
        copies[1 + piece].wait()
        rows = x_ref[:, max(8192 * piece - 128, 0) : min(8192 * piece + 8320, 32768)]
        if piece == 0:
            rows = jnp.concatenate([edge, rows], axis=1)
        if piece == 3:
            rows = jnp.concatenate([rows, edge], axis=1)
        windows = jnp.concatenate(
            [part[:, 512 * b : 512 * b + 768] for part in split_rows(rows, 3) for b in range(16)],
            axis=0,
        )
        product = jnp.dot(windows, fir_ref[...], preferred_element_type=F32)
        decimated = product[0:256, :128] + (
            product[0:256, 128:]
            + (product[256:512, :128] + (product[256:512, 128:] + product[512:768, :128]))
        )
        for b in range(16):
            segment, part = 2 * piece + b // 8, b % 8
            seg_ref[segment * OWN : (segment + 1) * OWN, part * 128 : (part + 1) * 128] = (
                decimated[b * OWN : (b + 1) * OWN]
            )
    copies[5].wait()
    copies[6].wait()
    rows = SEG * OWN
    first, second = seg_ref[:, : NT // 2], seg_ref[:, NT // 2 :]
    halves = []
    for parity, folded in enumerate((first + second, first - second)):
        terms = jnp.concatenate(split_rows(folded, 3), axis=0)
        high = jnp.dot(terms, dft_ref[parity, 0], preferred_element_type=F32)
        mid = jnp.dot(terms[: 2 * rows], dft_ref[parity, 1], preferred_element_type=F32)
        low = jnp.dot(terms[:rows], dft_ref[parity, 2], preferred_element_type=F32)
        halves.append(
            high[:rows] + (high[rows : 2 * rows] + mid[:rows] + (high[2 * rows :] + mid[rows:] + low))
        )
    cut = NBINS // 2
    real_part = jnp.concatenate([halves[0][:, :cut], halves[1][:, :cut]], axis=1)
    imag_part = jnp.concatenate([halves[0][:, cut:], halves[1][:, cut:]], axis=1)
    power = real_part * real_part + imag_part * imag_part
    sums = jnp.dot(
        jnp.concatenate(split_rows(power, 2), axis=0), smooth_ref[...], preferred_element_type=F32
    )
    level = (sums[:rows] + sums[rows:]) / 65.0
    own_ids = base_ref[0] + (lax.broadcasted_iota(jnp.int32, (rows, 32), 0) & (OWN - 1))
    dead = jnp.max(jnp.where(dead_ref[...] == own_ids, 1.0, 0.0), axis=1, keepdims=True)
    scale = lax.rsqrt(level + 1e-06) * (1.0 - dead)
    real_part = real_part * scale
    imag_part = imag_part * scale
    for segment in range(SEG):
        take = slice(segment * OWN, (segment + 1) * OWN)
        for col in range(NBINS // 128):
            lanes = slice(col * 128, (col + 1) * 128)
            turn_ref[col, pl.ds(segment, OWN, stride=2 * SEG), :] = real_part[take, lanes]
            turn_ref[col, pl.ds(SEG + segment, OWN, stride=2 * SEG), :] = imag_part[take, lanes]
    for col in range(NBINS // 128):
        turned = turn_ref[col].reshape(OWN, 2 * SEG, 128).astype(BF16)
        for copy in range(GROUP):
            out_ref[copy, :, :, col * 128 : (col + 1) * 128] = turned


def pick_kernel(place_ref, sources_ref, line_ref, out_ref):
    for spot in range(PLANE):
        side, core, block = spot // 16, spot // 8 % 2, spot % 8
        index = 4 * ((block // 4) * 16 + (block % 4) * 4 + place_ref[0]) + core * 2 + side
        out_ref[spot] = line_ref[sources_ref[index] & (LINE - 1)]


def hold_kernel(owner_ref, arrived_ref, out_ref):
    held = arrived_ref[owner_ref[0]]
    for spot in range(SLOTS):
        out_ref[spot] = held


def ready_kernel(line_ref, chan_ref):
    cols = NBINS // 128
    for channel in range(LINE):
        wide = line_ref[channel].astype(F32)
        real_part, imag_part = wide[:SEG], wide[SEG:]
        for kind, rows in enumerate((real_part, real_part - imag_part, real_part + imag_part)):
            for col in range(cols):
                first = (kind * cols + col) * SEG * LINE + channel
                chan_ref[pl.ds(first, SEG, stride=LINE), :] = rows[:, col * 128 : (col + 1) * 128]


def corr_kernel(source_ref, own_ref, sibling_ref, lag_ref, out_ref, src_ref, cross_ref):
    cols = NBINS // 128
    wide = source_ref[...].astype(F32)
    src_ref[:, 0:SEG] = wide[:, 0:SEG] + wide[:, SEG:]
    src_ref[:, SEG : 2 * SEG] = wide[:, SEG:]
    src_ref[:, 2 * SEG :] = wide[:, 0:SEG]

    def step(index, carry):
        pair, tile = index // 4, index % 4
        for col in range(cols):
            lanes = slice(col * 128, (col + 1) * 128)
            for half, chan_ref in enumerate((own_ref, sibling_ref)):

                def sums(kind):
                    totals = [None] * 4
                    for segment in range(SEG):
                        first = ((kind * cols + col) * SEG + segment) * LINE + tile * 16
                        channel_rows = chan_ref[pl.ds(pl.multiple_of(first, 16), 16), :]
                        for member in range(4):
                            slot = (member % 2) * 8 + 2 * pair + member // 2
                            row = src_ref[slot, pl.ds(kind * SEG + segment, 1), lanes]
                            term = row * channel_rows
                            old = totals[member]
                            totals[member] = term if old is None else old + term
                    return totals

                common = sums(0)
                for kind in (1, 2):
                    other = sums(kind)
                    spot = (kind - 1) * NBINS + col * 128
                    for member in range(4):
                        first = (4 * pair + member) * 2 * LINE + half * LINE + tile * 16
                        cross_ref[pl.ds(pl.multiple_of(first, 16), 16), spot : spot + 128] = (
                            common[member] - other[member]
                        ).astype(BF16)
        return carry

    lax.fori_loop(0, 16, step, 0)
    for half in range(2):
        pairs = SLOTS * LINE
        result = lax.dot_general(
            lag_ref[...],
            cross_ref[half * pairs : (half + 1) * pairs],
            (((1,), (1,)), ((), ())),
            preferred_element_type=F32,
        ).astype(BF16)
        for block in range(4):
            for part in range(4):
                out_ref[part, 4 * half + block] = result[
                    part * 64 : (part + 1) * 64, block * 4 * LINE : (block + 1) * 4 * LINE
                ]


def spread_kernel(in_ref, out_ref):
    for core in range(2):
        for far in range(2):
            for pair in range(2):
                left = in_ref[0, core, far, 2 * pair].astype(F32)
                right = in_ref[0, core, far, 2 * pair + 1].astype(F32)
                for part in range(4):
                    side, half = part // 2, part % 2
                    lanes = slice(part * LINE, (part + 1) * LINE)
                    spot = (core ^ half) * 512 + far * 256 + pair * 128
                    out_ref[2 * core + side, :, spot : spot + 128] = jnp.concatenate(
                        [left[:, lanes], right[:, lanes]], axis=1
                    )


def vmem():
    return pl.BlockSpec(memory_space=pltpu.VMEM)


def smem():
    return pl.BlockSpec(memory_space=pltpu.SMEM)


def whole():
    return pl.BlockSpec(memory_space=pl.ANY)


SMALL = pltpu.CompilerParams(vmem_limit_bytes=12 * 1024 * 1024)
MEDIUM = pltpu.CompilerParams(vmem_limit_bytes=24 * 1024 * 1024)
FULL = pltpu.CompilerParams(vmem_limit_bytes=60 * 1024 * 1024)


def call_whiten(base, records, dead_list):
    return pl.pallas_call(
        whiten_kernel,
        out_shape=jax.ShapeDtypeStruct((GROUP, OWN, 2 * SEG, NBINS), BF16),
        in_specs=[smem(), whole(), whole(), whole(), whole(), vmem()],
        out_specs=vmem(),
        scratch_shapes=[
            pltpu.VMEM((OWN, 32768), F32),
            pltpu.VMEM((768, 256), BF16),
            pltpu.VMEM((2, 3, NT // 2, NBINS), BF16),
            pltpu.VMEM((NBINS, NBINS), BF16),
            pltpu.VMEM((SEG * OWN, NT), F32),
            pltpu.VMEM((NBINS // 128, OWN * 2 * SEG, 128), F32),
            pltpu.SemaphoreType.DMA((7,)),
        ],
        compiler_params=FULL,
        name="whiten",
    )(
        base,
        records,
        jnp.asarray(fir_table()),
        jnp.asarray(dft_table()),
        jnp.asarray(smooth_table()),
        dead_list.reshape(1, 32),
    )


def call_pick(place, sources, line):
    return pl.pallas_call(
        pick_kernel,
        out_shape=jax.ShapeDtypeStruct((PLANE, 2 * SEG, NBINS), BF16),
        in_specs=[smem(), smem(), vmem()],
        out_specs=vmem(),
        compiler_params=SMALL,
        name="pick",
    )(place, sources, line)


def call_hold(owner, arrived):
    return pl.pallas_call(
        hold_kernel,
        out_shape=jax.ShapeDtypeStruct((SLOTS, 2 * SEG, NBINS), BF16),
        in_specs=[smem(), vmem()],
        out_specs=vmem(),
        compiler_params=SMALL,
        name="hold",
    )(owner, arrived)


def call_ready(line):
    return pl.pallas_call(
        ready_kernel,
        out_shape=jax.ShapeDtypeStruct((3 * NBINS // 128 * LINE * SEG, 128), F32),
        in_specs=[vmem()],
        out_specs=vmem(),
        compiler_params=SMALL,
        cost_estimate=pl.CostEstimate(flops=2000000, bytes_accessed=8388608, transcendentals=0),
        name="ready",
    )(line)


def call_corr(source_spectra, own, sibling):
    return pl.pallas_call(
        corr_kernel,
        out_shape=jax.ShapeDtypeStruct((4, 8, LAGS // 4, 4 * LINE), BF16),
        in_specs=[vmem(), vmem(), vmem(), vmem()],
        out_specs=vmem(),
        scratch_shapes=[
            pltpu.VMEM((SLOTS, 3 * SEG, NBINS), F32),
            pltpu.VMEM((PLANE * LINE, 2 * NBINS), BF16),
        ],
        compiler_params=MEDIUM,
        name="correlate",
    )(source_spectra, own, sibling, jnp.asarray(lag_table()))


def call_spread(gathered):
    return pl.pallas_call(
        spread_kernel,
        grid=(2, 2),
        out_shape=jax.ShapeDtypeStruct((4, LAGS // 4, PLANE * LINE), F32),
        in_specs=[
            pl.BlockSpec((1, 2, 2, 4, LAGS // 8, 4 * LINE), lambda i, j: (i, 0, 0, 0, j, 0))
        ],
        out_specs=pl.BlockSpec((4, LAGS // 8, 16 * LINE), lambda i, j: (0, j, i)),
        compiler_params=SMALL,
        name="spread",
    )(gathered)


def shards(records, sources, dead_list):
    xl_pos = lax.axis_index("xl")
    core_pos = lax.axis_index("core")
    xh_pos = lax.axis_index("xh")
    z_pos = lax.axis_index("z")
    y_pos = lax.axis_index("y")
    chan_pos = (xh_pos * 4 + z_pos) * 4 + y_pos
    device = (xl_pos * 2 + core_pos) * 32 + chan_pos
    own_slot = sources[4 * chan_pos + core_pos * 2 + xl_pos]
    whitened = call_whiten((device * OWN).reshape(1), records, dead_list)
    line = lax.all_to_all(whitened, "y", 0, 0, tiled=True).reshape(LINE, 2 * SEG, NBINS)
    sibling_line = lax.ppermute(line, "core", [(0, 1), (1, 0)])
    picked = call_pick(y_pos.reshape(1), sources, line)
    arrived = lax.all_to_all(picked, PLANE_AXES, 0, 0, tiled=True)
    held = call_hold((own_slot >> 6).reshape(1), arrived)
    source_spectra = lax.all_to_all(held, SIDE_AXES, 0, 0, tiled=True)
    blocks = call_corr(source_spectra, call_ready(line), call_ready(sibling_line))
    gathered = lax.all_to_all(
        blocks.reshape(PLANE, LAGS // 4, 4 * LINE), PLANE_AXES, 0, 0, tiled=True
    )
    return call_spread(gathered.reshape(2, 2, 2, 4, LAGS // 4, 4 * LINE))


def solution(mesh):
    inner = Mesh(mesh.devices.reshape(2, 2, 2, 4, 4), AXES)
    return jax.shard_map(
        shards,
        mesh=inner,
        in_specs=(P(AXES, None), P(), P()),
        out_specs=P(("xh", "z", "y"), ("xl", "core"), None),
        check_vma=False,
    )
```

```python
import numpy as np
import jax
import jax.numpy as jnp
from jax import lax
from jax.experimental import pallas as pl
from jax.experimental.pallas import tpu as pltpu
from jax.sharding import Mesh, PartitionSpec as P

NT = 1024
LAGS = 256
SEG = 8
NBINS = 512
OWN = 16
GROUP = 4
PLANE = 32
LINE = GROUP * OWN
AXES = ("xl", "core", "xh", "z", "y")
PLANE_AXES = ("xl", "core", "xh", "z")
SIDE_AXES = ("xl", "xh", "z")
SLOTS = 16
WIDE = 2 * SEG * NBINS
UNROLL = 4
BIN_ORDER = np.concatenate([np.arange(2, NBINS + 1, 2), np.arange(1, NBINS, 2)])
PIECES = (0, 8320, 16512, 24704, 32768)
F32 = jnp.float32
BF16 = jnp.bfloat16


def split_table(table, terms):
    left = table.astype(np.float64)
    parts = []
    for _ in range(terms):
        part = left.astype(np.float32).astype(BF16)
        parts.append(part)
        left = left - part.astype(np.float64)
    return parts


def fir_table():
    row = np.arange(768)[:, None]
    col = np.arange(128)[None, :]
    offset = 4 * col + 255 - row
    inside = (offset >= 0) & (offset <= 254)
    tap = offset.astype(np.float64)
    hamming = 0.54 - 0.46 * np.cos(2.0 * np.pi * tap / 254.0)
    values = 0.2 * np.sinc(0.2 * (tap - 127.0)) * hamming
    return np.concatenate(split_table(np.where(inside, values, 0.0), 2), axis=1)


def dft_table():
    sample = np.arange(NT // 2)[:, None]
    tables = []
    for bins in (BIN_ORDER[: NBINS // 2], BIN_ORDER[NBINS // 2 :]):
        angle = (sample * bins[None, :] % NT) * (2.0 * np.pi / NT)
        table = np.concatenate([np.cos(angle), -np.sin(angle)], axis=1)
        tables.append(np.stack(split_table(table, 3)))
    return np.stack(tables)


def smooth_table():
    return (np.abs(BIN_ORDER[:, None] - BIN_ORDER[None, :]) <= 32).astype(BF16)


def lag_table():
    lags = (np.arange(LAGS) - LAGS // 2)[:, None]
    angle = (BIN_ORDER[None, :] * lags % NT) * (2.0 * np.pi / NT)
    groups = (LAGS, NBINS // 16, 16)
    table = np.stack([np.cos(angle).reshape(groups), -np.sin(angle).reshape(groups)], axis=2)
    return (table.reshape(LAGS, 2 * NBINS) / np.sqrt(SEG * NBINS)).astype(np.float32).astype(BF16)


def split_rows(value, terms):
    parts = []
    for term in range(terms):
        part = value.astype(BF16)
        parts.append(part)
        if term < terms - 1:
            value = value - part.astype(F32)
    return parts


def whiten_kernel(
    base_ref, x_hbm, fir_hbm, dft_hbm, smooth_hbm, dead_ref, out_ref,
    x_ref, fir_ref, dft_ref, smooth_ref, seg_ref, sems,
):
    copies = [pltpu.make_async_copy(fir_hbm, fir_ref, sems.at[0])]
    for piece in range(4):
        lanes = pl.ds(PIECES[piece], PIECES[piece + 1] - PIECES[piece])
        copies.append(
            pltpu.make_async_copy(x_hbm.at[:, lanes], x_ref.at[:, lanes], sems.at[1 + piece])
        )
    copies.append(pltpu.make_async_copy(dft_hbm, dft_ref, sems.at[5]))
    copies.append(pltpu.make_async_copy(smooth_hbm, smooth_ref, sems.at[6]))
    for copy in copies:
        copy.start()
    copies[0].wait()
    edge = jnp.zeros((OWN, 128), F32)
    for piece in range(4):
        copies[1 + piece].wait()
        rows = x_ref[:, max(8192 * piece - 128, 0) : min(8192 * piece + 8320, 32768)]
        if piece == 0:
            rows = jnp.concatenate([edge, rows], axis=1)
        if piece == 3:
            rows = jnp.concatenate([rows, edge], axis=1)
        windows = jnp.concatenate(
            [part[:, 512 * b : 512 * b + 768] for part in split_rows(rows, 3) for b in range(16)],
            axis=0,
        )
        product = jnp.dot(windows, fir_ref[...], preferred_element_type=F32)
        decimated = product[0:256, :128] + (
            product[0:256, 128:]
            + (product[256:512, :128] + (product[256:512, 128:] + product[512:768, :128]))
        )
        for b in range(16):
            segment, part = 2 * piece + b // 8, b % 8
            seg_ref[segment * OWN : (segment + 1) * OWN, part * 128 : (part + 1) * 128] = (
                decimated[b * OWN : (b + 1) * OWN]
            )
    copies[5].wait()
    copies[6].wait()
    rows = SEG * OWN
    first, second = seg_ref[:, : NT // 2], seg_ref[:, NT // 2 :]
    halves = []
    for parity, folded in enumerate((first + second, first - second)):
        terms = jnp.concatenate(split_rows(folded, 3), axis=0)
        high = jnp.dot(terms, dft_ref[parity, 0], preferred_element_type=F32)
        mid = jnp.dot(terms[: 2 * rows], dft_ref[parity, 1], preferred_element_type=F32)
        low = jnp.dot(terms[:rows], dft_ref[parity, 2], preferred_element_type=F32)
        halves.append(
            high[:rows] + (high[rows : 2 * rows] + mid[:rows] + (high[2 * rows :] + mid[rows:] + low))
        )
    cut = NBINS // 2
    real_part = jnp.concatenate([halves[0][:, :cut], halves[1][:, :cut]], axis=1)
    imag_part = jnp.concatenate([halves[0][:, cut:], halves[1][:, cut:]], axis=1)
    power = real_part * real_part + imag_part * imag_part
    sums = jnp.dot(
        jnp.concatenate(split_rows(power, 2), axis=0), smooth_ref[...], preferred_element_type=F32
    )
    level = (sums[:rows] + sums[rows:]) / 65.0
    own_ids = base_ref[0] + (lax.broadcasted_iota(jnp.int32, (rows, 32), 0) & (OWN - 1))
    dead = jnp.max(jnp.where(dead_ref[...] == own_ids, 1.0, 0.0), axis=1, keepdims=True)
    scale = lax.rsqrt(level + 1e-06) * (1.0 - dead)
    real_part = real_part * scale
    imag_part = imag_part * scale
    chunk = lax.broadcasted_iota(jnp.int32, (OWN, 128), 1) >> 4
    for kind, part in enumerate((real_part, imag_part)):
        for col in range(NBINS // 128):
            lanes = slice(col * 128, (col + 1) * 128)
            tiles = [part[s * OWN : (s + 1) * OWN, lanes] for s in range(SEG)]
            for step in (1, 2, 4):
                low = (chunk & step) == 0
                for s in range(SEG):
                    if s & step == 0:
                        upper, lower = tiles[s], tiles[s + step]
                        tiles[s] = jnp.where(low, upper, pltpu.roll(lower, 16 * step, 1))
                        tiles[s + step] = jnp.where(low, pltpu.roll(upper, 128 - 16 * step, 1), lower)
            for member in range(SEG):
                first = (col * SEG + member) * 256 + kind * 128
                turned = tiles[member].astype(BF16)
                for copy in range(GROUP):
                    out_ref[copy, :, first : first + 128] = turned


def pick_kernel(place_ref, sources_ref, line_ref, out_ref, wide_ref):
    for tile in range(WIDE // 128):
        wide_ref[tile * LINE : (tile + 1) * LINE] = line_ref[
            :, tile * 128 : (tile + 1) * 128
        ].astype(F32)
    for spot in range(PLANE):
        side, core, block = spot // 16, spot // 8 % 2, spot % 8
        index = 4 * ((block // 4) * 16 + (block % 4) * 4 + place_ref[0]) + core * 2 + side
        channel = sources_ref[index] & (LINE - 1)
        for col in range(4):
            rows = pl.ds(col * LINE + channel, 16, stride=4 * LINE)
            out_ref[spot, :, col * 128 : (col + 1) * 128] = wide_ref[rows, :].astype(BF16)


def hold_kernel(owner_ref, arrived_ref, out_ref):
    held = arrived_ref[owner_ref[0]]
    for spot in range(SLOTS):
        out_ref[spot] = held


def corr_kernel(
    source_ref, own_hbm, sibling_hbm, lag_hbm, out_ref,
    line_ref, lag_ref, src_ref, cross_ref, sems,
):
    copies = []
    for half in range(2):
        lanes = pl.ds(half * WIDE // 2, WIDE // 2)
        for core, line_hbm in enumerate((own_hbm, sibling_hbm)):
            copies.append(
                pltpu.make_async_copy(
                    line_hbm.at[:, lanes],
                    line_ref.at[core * LINE : (core + 1) * LINE, lanes],
                    sems.at[2 * half + core],
                )
            )
    copies.append(pltpu.make_async_copy(lag_hbm, lag_ref, sems.at[4]))
    for copy in copies:
        copy.start()
    src_ref[...] = source_ref[...].astype(F32)
    row = lax.broadcasted_iota(jnp.int32, (16, 256), 0)
    lane = lax.broadcasted_iota(jnp.int32, (16, 256), 1)
    real_mask = jnp.where(row == (lane & 15), 1.0, 0.0)
    imag_mask = jnp.where(lane < 128, real_mask, -real_mask)

    def group_step(line_row, side):
        group = line_row * 2 + side
        spread = []
        for slot in range(SLOTS):
            values = src_ref[slot, pl.ds(line_row, 1), side * 256 : (side + 1) * 256]
            swapped = jnp.concatenate([values[:, 128:], values[:, :128]], axis=1)
            spread.append((real_mask * values).astype(BF16))
            spread.append((imag_mask * swapped).astype(BF16))
        lanes = pl.ds(pl.multiple_of(group * 256, 256), 256)
        cross = lax.dot_general(
            jnp.concatenate(spread, axis=0),
            line_ref[:, lanes],
            (((1,), (1,)), ((), ())),
            preferred_element_type=F32,
        ).astype(BF16)
        rows = pl.ds(pl.multiple_of(group * 32, 32), 32)
        for slot in range(SLOTS):
            cross_ref[rows, slot * 128 : (slot + 1) * 128] = cross[slot * 32 : (slot + 1) * 32]

    def step(index, carry):
        for inner in range(UNROLL):
            for side in range(2):
                group_step(index * UNROLL + inner, side)
        return carry

    for half in range(2):
        copies[2 * half].wait()
        copies[2 * half + 1].wait()
        lax.fori_loop(half * 8 // UNROLL, (half + 1) * 8 // UNROLL, step, 0)
    copies[4].wait()
    for side in range(2):
        lanes = slice(side * 1024, (side + 1) * 1024)
        result = jnp.dot(
            lag_ref[...], cross_ref[:, lanes], preferred_element_type=F32
        ).astype(BF16)
        for block in range(8):
            for part in range(4):
                out_ref[part, block, :, side * 128 : (side + 1) * 128] = result[
                    part * 64 : (part + 1) * 64, block * 128 : (block + 1) * 128
                ]


def spread_kernel(in_ref, out_ref):
    for core in range(2):
        for far in range(2):
            for pair in range(2):
                left = in_ref[0, core, far, 2 * pair].astype(F32)
                right = in_ref[0, core, far, 2 * pair + 1].astype(F32)
                for part in range(4):
                    side, half = part // 2, part % 2
                    lanes = slice(part * LINE, (part + 1) * LINE)
                    spot = (core ^ half) * 512 + far * 256 + pair * 128
                    out_ref[2 * core + side, :, spot : spot + 128] = jnp.concatenate(
                        [left[:, lanes], right[:, lanes]], axis=1
                    )


def vmem():
    return pl.BlockSpec(memory_space=pltpu.VMEM)


def smem():
    return pl.BlockSpec(memory_space=pltpu.SMEM)


def whole():
    return pl.BlockSpec(memory_space=pl.ANY)


SMALL = pltpu.CompilerParams(vmem_limit_bytes=12 * 1024 * 1024)
FULL = pltpu.CompilerParams(vmem_limit_bytes=60 * 1024 * 1024)


def call_whiten(base, records, dead_list):
    return pl.pallas_call(
        whiten_kernel,
        out_shape=jax.ShapeDtypeStruct((GROUP, OWN, WIDE), BF16),
        in_specs=[smem(), whole(), whole(), whole(), whole(), vmem()],
        out_specs=vmem(),
        scratch_shapes=[
            pltpu.VMEM((OWN, 32768), F32),
            pltpu.VMEM((768, 256), BF16),
            pltpu.VMEM((2, 3, NT // 2, NBINS), BF16),
            pltpu.VMEM((NBINS, NBINS), BF16),
            pltpu.VMEM((SEG * OWN, NT), F32),
            pltpu.SemaphoreType.DMA((7,)),
        ],
        compiler_params=FULL,
        name="whiten",
    )(
        base,
        records,
        jnp.asarray(fir_table()),
        jnp.asarray(dft_table()),
        jnp.asarray(smooth_table()),
        dead_list.reshape(1, 32),
    )


def call_pick(place, sources, line):
    return pl.pallas_call(
        pick_kernel,
        out_shape=jax.ShapeDtypeStruct((PLANE, 2 * SEG, NBINS), BF16),
        in_specs=[smem(), smem(), vmem()],
        out_specs=vmem(),
        scratch_shapes=[pltpu.VMEM((WIDE // 128 * LINE, 128), F32)],
        compiler_params=SMALL,
        name="pick",
    )(place, sources, line)


def call_hold(owner, arrived):
    return pl.pallas_call(
        hold_kernel,
        out_shape=jax.ShapeDtypeStruct((SLOTS, 2 * SEG, NBINS), BF16),
        in_specs=[smem(), vmem()],
        out_specs=vmem(),
        compiler_params=SMALL,
        name="hold",
    )(owner, arrived)


def call_corr(source_spectra, own, sibling):
    return pl.pallas_call(
        corr_kernel,
        out_shape=jax.ShapeDtypeStruct((4, 8, LAGS // 4, 4 * LINE), BF16),
        in_specs=[vmem(), whole(), whole(), whole()],
        out_specs=vmem(),
        scratch_shapes=[
            pltpu.VMEM((2 * LINE, WIDE), BF16),
            pltpu.VMEM((LAGS, 2 * NBINS), BF16),
            pltpu.VMEM((SLOTS, 16, 512), F32),
            pltpu.VMEM((2 * NBINS, SLOTS * 2 * LINE), BF16),
            pltpu.SemaphoreType.DMA((5,)),
        ],
        compiler_params=FULL,
        name="correlate",
    )(source_spectra, own, sibling, jnp.asarray(lag_table()))


def call_spread(gathered):
    return pl.pallas_call(
        spread_kernel,
        grid=(2,),
        out_shape=jax.ShapeDtypeStruct((4, LAGS // 4, PLANE * LINE), F32),
        in_specs=[
            pl.BlockSpec((1, 2, 2, 4, LAGS // 4, 4 * LINE), lambda i: (i, 0, 0, 0, 0, 0))
        ],
        out_specs=pl.BlockSpec((4, LAGS // 4, 16 * LINE), lambda i: (0, 0, i)),
        compiler_params=SMALL,
        name="spread",
    )(gathered)


def shards(records, sources, dead_list):
    xl_pos = lax.axis_index("xl")
    core_pos = lax.axis_index("core")
    xh_pos = lax.axis_index("xh")
    z_pos = lax.axis_index("z")
    y_pos = lax.axis_index("y")
    chan_pos = (xh_pos * 4 + z_pos) * 4 + y_pos
    device = (xl_pos * 2 + core_pos) * 32 + chan_pos
    own_slot = sources[4 * chan_pos + core_pos * 2 + xl_pos]
    whitened = call_whiten((device * OWN).reshape(1), records, dead_list)
    line = lax.all_to_all(whitened, "y", 0, 0, tiled=True).reshape(LINE, WIDE)
    sibling_line = lax.ppermute(line, "core", [(0, 1), (1, 0)])
    picked = call_pick(y_pos.reshape(1), sources, line)
    arrived = lax.all_to_all(picked, PLANE_AXES, 0, 0, tiled=True)
    held = call_hold((own_slot >> 6).reshape(1), arrived)
    source_spectra = lax.all_to_all(held, SIDE_AXES, 0, 0, tiled=True)
    blocks = call_corr(source_spectra, line, sibling_line)
    gathered = lax.all_to_all(
        blocks.reshape(PLANE, LAGS // 4, 4 * LINE), PLANE_AXES, 0, 0, tiled=True
    )
    return call_spread(gathered.reshape(2, 2, 2, 4, LAGS // 4, 4 * LINE))


def solution(mesh):
    inner = Mesh(mesh.devices.reshape(2, 2, 2, 4, 4), AXES)
    return jax.shard_map(
        shards,
        mesh=inner,
        in_specs=(P(AXES, None), P(), P()),
        out_specs=P(("xh", "z", "y"), ("xl", "core"), None),
        check_vma=False,
    )
```

```python
import numpy as np
import jax
import jax.numpy as jnp
from jax import lax
from jax.experimental import pallas as pl
from jax.experimental.pallas import tpu as pltpu
from jax.sharding import Mesh, PartitionSpec as P

NT = 1024
LAGS = 256
SEG = 8
NBINS = 512
OWN = 16
GROUP = 4
PLANE = 32
LINE = GROUP * OWN
AXES = ("xl", "core", "xh", "z", "y")
PLANE_AXES = ("xl", "core", "xh", "z")
SIDE_AXES = ("xl", "xh", "z")
SLOTS = 16
WIDE = 2 * SEG * NBINS
UNROLL = 4
PITCH = LINE + 1
BIN_ORDER = np.concatenate([np.arange(2, NBINS + 1, 2), np.arange(1, NBINS, 2)])
PIECES = (0, 8320, 16512, 24704, 32768)
F32 = jnp.float32
BF16 = jnp.bfloat16


def split_table(table, terms):
    left = table.astype(np.float64)
    parts = []
    for _ in range(terms):
        part = left.astype(np.float32).astype(BF16)
        parts.append(part)
        left = left - part.astype(np.float64)
    return parts


def fir_table():
    row = np.arange(768)[:, None]
    col = np.arange(128)[None, :]
    offset = 4 * col + 255 - row
    inside = (offset >= 0) & (offset <= 254)
    tap = offset.astype(np.float64)
    hamming = 0.54 - 0.46 * np.cos(2.0 * np.pi * tap / 254.0)
    values = np.where(inside, 0.2 * np.sinc(0.2 * (tap - 127.0)) * hamming, 0.0)
    outer = np.concatenate([values[:256, :64], values[512:, 64:]], axis=1)
    return np.concatenate(
        [np.concatenate(split_table(part, 2), axis=1) for part in (outer, values[256:512])], axis=0
    )


def dft_table():
    sample = np.arange(NT // 2)[:, None]
    tables = []
    for bins in (BIN_ORDER[: NBINS // 2], BIN_ORDER[NBINS // 2 :]):
        angle = (sample * bins[None, :] % NT) * (2.0 * np.pi / NT)
        table = np.concatenate([np.cos(angle), -np.sin(angle)], axis=1)
        tables.append(np.stack(split_table(table, 3)))
    return np.stack(tables)


def smooth_table():
    return (np.abs(BIN_ORDER[:, None] - BIN_ORDER[None, :]) <= 32).astype(BF16)


def lag_table():
    lags = (np.arange(LAGS) - LAGS // 2)[:, None]
    angle = (BIN_ORDER[None, :] * lags % NT) * (2.0 * np.pi / NT)
    groups = (LAGS, NBINS // 16, 16)
    table = np.stack([np.cos(angle).reshape(groups), -np.sin(angle).reshape(groups)], axis=2)
    return (table.reshape(LAGS, 2 * NBINS) / np.sqrt(SEG * NBINS)).astype(np.float32).astype(BF16)


def split_rows(value, terms):
    parts = []
    for term in range(terms):
        part = value.astype(BF16)
        parts.append(part)
        if term < terms - 1:
            value = value - part.astype(F32)
    return parts


def whiten_kernel(
    base_ref, x_hbm, fir_hbm, dft_hbm, smooth_hbm, dead_ref, out_ref,
    x_ref, fir_ref, dft_ref, smooth_ref, seg_ref, sems,
):
    copies = [pltpu.make_async_copy(fir_hbm, fir_ref, sems.at[0])]
    for piece in range(4):
        lanes = pl.ds(PIECES[piece], PIECES[piece + 1] - PIECES[piece])
        copies.append(
            pltpu.make_async_copy(x_hbm.at[:, lanes], x_ref.at[:, lanes], sems.at[1 + piece])
        )
    copies.append(pltpu.make_async_copy(dft_hbm, dft_ref, sems.at[5]))
    copies.append(pltpu.make_async_copy(smooth_hbm, smooth_ref, sems.at[6]))
    for copy in copies[:5]:
        copy.start()
    copies[0].wait()
    edge = jnp.zeros((OWN, 128), F32)
    left_lanes = lax.broadcasted_iota(jnp.int32, (16 * OWN, 128), 1) < 64

    def filtered(parts, first, blocks, table):
        count = blocks * OWN
        windows = jnp.concatenate(
            [part[:, first + 512 * b : first + 512 * b + 256] for part in parts for b in range(blocks)],
            axis=0,
        )
        product = jnp.dot(windows, table, preferred_element_type=F32)
        return product[:count, :128] + (
            product[:count, 128:]
            + (
                product[count : 2 * count, :128]
                + (product[count : 2 * count, 128:] + product[2 * count :, :128])
            )
        )

    for piece in range(4):
        copies[1 + piece].wait()
        if piece == 1:
            copies[5].start()
            copies[6].start()
        rows = x_ref[:, max(8192 * piece - 128, 0) : min(8192 * piece + 8320, 32768)]
        if piece == 0:
            rows = jnp.concatenate([edge, rows], axis=1)
        if piece == 3:
            rows = jnp.concatenate([rows, edge], axis=1)
        parts = split_rows(rows, 3)
        outer = filtered(parts, 0, 17, fir_ref[0:256])
        inner = filtered(parts, 256, 16, fir_ref[256:512])
        decimated = inner + jnp.where(left_lanes, outer[: 16 * OWN], outer[OWN:])
        for b in range(16):
            segment, part = 2 * piece + b // 8, b % 8
            seg_ref[segment * OWN : (segment + 1) * OWN, part * 128 : (part + 1) * 128] = (
                decimated[b * OWN : (b + 1) * OWN]
            )
    copies[5].wait()
    copies[6].wait()
    rows = SEG * OWN
    first, second = seg_ref[:, : NT // 2], seg_ref[:, NT // 2 :]
    halves = []
    for parity, folded in enumerate((first + second, first - second)):
        terms = jnp.concatenate(split_rows(folded, 3), axis=0)
        high = jnp.dot(terms, dft_ref[parity, 0], preferred_element_type=F32)
        mid = jnp.dot(terms[: 2 * rows], dft_ref[parity, 1], preferred_element_type=F32)
        low = jnp.dot(terms[:rows], dft_ref[parity, 2], preferred_element_type=F32)
        halves.append(
            high[:rows] + (high[rows : 2 * rows] + mid[:rows] + (high[2 * rows :] + mid[rows:] + low))
        )
    cut = NBINS // 2
    real_part = jnp.concatenate([halves[0][:, :cut], halves[1][:, :cut]], axis=1)
    imag_part = jnp.concatenate([halves[0][:, cut:], halves[1][:, cut:]], axis=1)
    power = real_part * real_part + imag_part * imag_part
    sums = jnp.dot(
        jnp.concatenate(split_rows(power, 2), axis=0), smooth_ref[...], preferred_element_type=F32
    )
    level = (sums[:rows] + sums[rows:]) / 65.0
    own_ids = base_ref[0] + (lax.broadcasted_iota(jnp.int32, (rows, 32), 0) & (OWN - 1))
    dead = jnp.max(jnp.where(dead_ref[...] == own_ids, 1.0, 0.0), axis=1, keepdims=True)
    scale = lax.rsqrt(level + 1e-06) * (1.0 - dead)
    real_part = real_part * scale
    imag_part = imag_part * scale
    chunk = lax.broadcasted_iota(jnp.int32, (OWN, 128), 1) >> 4
    for kind, part in enumerate((real_part, imag_part)):
        for col in range(NBINS // 128):
            lanes = slice(col * 128, (col + 1) * 128)
            tiles = [part[s * OWN : (s + 1) * OWN, lanes] for s in range(SEG)]
            for step in (1, 2, 4):
                low = (chunk & step) == 0
                for s in range(SEG):
                    if s & step == 0:
                        upper, lower = tiles[s], tiles[s + step]
                        tiles[s] = jnp.where(low, upper, pltpu.roll(lower, 16 * step, 1))
                        tiles[s + step] = jnp.where(low, pltpu.roll(upper, 128 - 16 * step, 1), lower)
            for member in range(SEG):
                first = (col * SEG + member) * 256 + kind * 128
                turned = tiles[member].astype(BF16)
                for copy in range(GROUP):
                    out_ref[copy, :, first : first + 128] = turned


def pick_kernel(place_ref, sources_ref, line_ref, out_ref, wide_ref):
    for tile in range(WIDE // 128):
        first = tile // 4 * PITCH
        wide_ref[tile % 4, first : first + LINE] = line_ref[
            :, tile * 128 : (tile + 1) * 128
        ].astype(F32)
    for spot in range(PLANE):
        side, core, block = spot // 16, spot // 8 % 2, spot % 8
        index = 4 * ((block // 4) * 16 + (block % 4) * 4 + place_ref[0]) + core * 2 + side
        channel = sources_ref[index] & (LINE - 1)
        for col in range(4):
            rows = wide_ref[col, pl.ds(channel, 16, stride=PITCH), :]
            out_ref[spot, :, col * 128 : (col + 1) * 128] = rows.astype(BF16)


def hold_kernel(owner_ref, arrived_ref, out_ref):
    held = arrived_ref[owner_ref[0]]
    for spot in range(SLOTS):
        out_ref[spot] = held


def corr_kernel(source_ref, own_ref, sibling_ref, lag_ref, out_ref, src_ref, cross_ref):
    src_ref[...] = source_ref[...].astype(F32)
    row = lax.broadcasted_iota(jnp.int32, (16, 256), 0)
    lane = lax.broadcasted_iota(jnp.int32, (16, 256), 1)
    real_mask = jnp.where(row == (lane & 15), 1.0, 0.0)
    imag_mask = jnp.where(lane < 128, real_mask, -real_mask)

    def group_step(line_row, side):
        group = line_row * 2 + side
        spread = []
        for slot in range(SLOTS):
            values = src_ref[slot, pl.ds(line_row, 1), side * 256 : (side + 1) * 256]
            swapped = jnp.concatenate([values[:, 128:], values[:, :128]], axis=1)
            spread.append((real_mask * values).astype(BF16))
            spread.append((imag_mask * swapped).astype(BF16))
        lanes = pl.ds(pl.multiple_of(group * 256, 256), 256)
        cross = lax.dot_general(
            jnp.concatenate(spread, axis=0),
            jnp.concatenate([own_ref[:, lanes], sibling_ref[:, lanes]], axis=0),
            (((1,), (1,)), ((), ())),
            preferred_element_type=F32,
        ).astype(BF16)
        rows = pl.ds(pl.multiple_of(group * 32, 32), 32)
        for slot in range(SLOTS):
            cross_ref[rows, slot * 128 : (slot + 1) * 128] = cross[slot * 32 : (slot + 1) * 32]

    def step(index, carry):
        for inner in range(UNROLL):
            for side in range(2):
                group_step(index * UNROLL + inner, side)
        return carry

    lax.fori_loop(0, 16 // UNROLL, step, 0)
    for side in range(2):
        lanes = slice(side * 1024, (side + 1) * 1024)
        result = jnp.dot(
            lag_ref[...], cross_ref[:, lanes], preferred_element_type=F32
        ).astype(BF16)
        for block in range(8):
            for part in range(4):
                out_ref[part, block, :, side * 128 : (side + 1) * 128] = result[
                    part * 64 : (part + 1) * 64, block * 128 : (block + 1) * 128
                ]


def spread_kernel(in_ref, out_ref):
    for core in range(2):
        for far in range(2):
            for pair in range(2):
                left = in_ref[0, core, far, 2 * pair].astype(F32)
                right = in_ref[0, core, far, 2 * pair + 1].astype(F32)
                for part in range(4):
                    side, half = part // 2, part % 2
                    lanes = slice(part * LINE, (part + 1) * LINE)
                    spot = (core ^ half) * 512 + far * 256 + pair * 128
                    out_ref[2 * core + side, :, spot : spot + 128] = jnp.concatenate(
                        [left[:, lanes], right[:, lanes]], axis=1
                    )


def vmem():
    return pl.BlockSpec(memory_space=pltpu.VMEM)


def smem():
    return pl.BlockSpec(memory_space=pltpu.SMEM)


def whole():
    return pl.BlockSpec(memory_space=pl.ANY)


SMALL = pltpu.CompilerParams(vmem_limit_bytes=12 * 1024 * 1024)
MEDIUM = pltpu.CompilerParams(vmem_limit_bytes=20 * 1024 * 1024)
FULL = pltpu.CompilerParams(vmem_limit_bytes=60 * 1024 * 1024)


def call_whiten(base, records, dead_list):
    return pl.pallas_call(
        whiten_kernel,
        out_shape=jax.ShapeDtypeStruct((GROUP, OWN, WIDE), BF16),
        in_specs=[smem(), whole(), whole(), whole(), whole(), vmem()],
        out_specs=vmem(),
        scratch_shapes=[
            pltpu.VMEM((OWN, 32768), F32),
            pltpu.VMEM((512, 256), BF16),
            pltpu.VMEM((2, 3, NT // 2, NBINS), BF16),
            pltpu.VMEM((NBINS, NBINS), BF16),
            pltpu.VMEM((SEG * OWN, NT), F32),
            pltpu.SemaphoreType.DMA((7,)),
        ],
        compiler_params=FULL,
        name="whiten",
    )(
        base,
        records,
        jnp.asarray(fir_table()),
        jnp.asarray(dft_table()),
        jnp.asarray(smooth_table()),
        dead_list.reshape(1, 32),
    )


def call_pick(place, sources, line):
    return pl.pallas_call(
        pick_kernel,
        out_shape=jax.ShapeDtypeStruct((PLANE, 2 * SEG, NBINS), BF16),
        in_specs=[smem(), smem(), vmem()],
        out_specs=vmem(),
        scratch_shapes=[pltpu.VMEM((4, 17 * LINE, 128), F32)],
        compiler_params=SMALL,
        name="pick",
    )(place, sources, line)


def call_hold(owner, arrived):
    return pl.pallas_call(
        hold_kernel,
        out_shape=jax.ShapeDtypeStruct((SLOTS, 2 * SEG, NBINS), BF16),
        in_specs=[smem(), vmem()],
        out_specs=vmem(),
        compiler_params=SMALL,
        name="hold",
    )(owner, arrived)


def call_corr(source_spectra, own, sibling):
    return pl.pallas_call(
        corr_kernel,
        out_shape=jax.ShapeDtypeStruct((4, 8, LAGS // 4, 4 * LINE), BF16),
        in_specs=[vmem(), vmem(), vmem(), vmem()],
        out_specs=vmem(),
        scratch_shapes=[
            pltpu.VMEM((SLOTS, 16, 512), F32),
            pltpu.VMEM((2 * NBINS, SLOTS * 2 * LINE), BF16),
        ],
        compiler_params=MEDIUM,
        name="correlate",
    )(source_spectra, own, sibling, jnp.asarray(lag_table()))


def call_spread(gathered):
    return pl.pallas_call(
        spread_kernel,
        grid=(2,),
        out_shape=jax.ShapeDtypeStruct((4, LAGS // 4, PLANE * LINE), F32),
        in_specs=[
            pl.BlockSpec((1, 2, 2, 4, LAGS // 4, 4 * LINE), lambda i: (i, 0, 0, 0, 0, 0))
        ],
        out_specs=pl.BlockSpec((4, LAGS // 4, 16 * LINE), lambda i: (0, 0, i)),
        compiler_params=SMALL,
        name="spread",
    )(gathered)


def shards(records, sources, dead_list):
    xl_pos = lax.axis_index("xl")
    core_pos = lax.axis_index("core")
    xh_pos = lax.axis_index("xh")
    z_pos = lax.axis_index("z")
    y_pos = lax.axis_index("y")
    chan_pos = (xh_pos * 4 + z_pos) * 4 + y_pos
    device = (xl_pos * 2 + core_pos) * 32 + chan_pos
    own_slot = sources[4 * chan_pos + core_pos * 2 + xl_pos]
    whitened = call_whiten((device * OWN).reshape(1), records, dead_list)
    line = lax.all_to_all(whitened, "y", 0, 0, tiled=True).reshape(LINE, WIDE)
    picked = call_pick(y_pos.reshape(1), sources, line)
    picked, sent_line = lax.optimization_barrier((picked, line))
    sibling_line = lax.ppermute(sent_line, "core", [(0, 1), (1, 0)])
    arrived = lax.all_to_all(picked, PLANE_AXES, 0, 0, tiled=True)
    held = call_hold((own_slot >> 6).reshape(1), arrived)
    source_spectra = lax.all_to_all(held, SIDE_AXES, 0, 0, tiled=True)
    blocks = call_corr(source_spectra, sent_line, sibling_line)
    gathered = lax.all_to_all(
        blocks.reshape(PLANE, LAGS // 4, 4 * LINE), PLANE_AXES, 0, 0, tiled=True
    )
    return call_spread(gathered.reshape(2, 2, 2, 4, LAGS // 4, 4 * LINE))


def solution(mesh):
    inner = Mesh(mesh.devices.reshape(2, 2, 2, 4, 4), AXES)
    return jax.shard_map(
        shards,
        mesh=inner,
        in_specs=(P(AXES, None), P(), P()),
        out_specs=P(("xh", "z", "y"), ("xl", "core"), None),
        check_vma=False,
    )
```

```python
import numpy as np
import jax
import jax.numpy as jnp
from jax import lax
from jax.experimental import pallas as pl
from jax.experimental.pallas import tpu as pltpu
from jax.sharding import Mesh, PartitionSpec as P

NT = 1024
LAGS = 256
SEG = 8
NBINS = 512
OWN = 16
GROUP = 4
PLANE = 32
LINE = GROUP * OWN
AXES = ("xl", "core", "xh", "z", "y")
PLANE_AXES = ("xl", "core", "xh", "z")
SIDE_AXES = ("xl", "xh", "z")
SLOTS = 16
WIDE = 2 * SEG * NBINS
PITCH = LINE + 1
BIN_ORDER = np.concatenate([np.arange(2, NBINS + 1, 2), np.arange(1, NBINS, 2)])
PIECES = (0, 8320, 16512, 24704, 32768)
F32 = jnp.float32
BF16 = jnp.bfloat16


def split_table(table, terms):
    left = table.astype(np.float64)
    parts = []
    for _ in range(terms):
        part = left.astype(np.float32).astype(BF16)
        parts.append(part)
        left = left - part.astype(np.float64)
    return parts


def fir_table():
    row = np.arange(768)[:, None]
    col = np.arange(128)[None, :]
    offset = 4 * col + 255 - row
    inside = (offset >= 0) & (offset <= 254)
    tap = offset.astype(np.float64)
    hamming = 0.54 - 0.46 * np.cos(2.0 * np.pi * tap / 254.0)
    values = np.where(inside, 0.2 * np.sinc(0.2 * (tap - 127.0)) * hamming, 0.0)
    outer = np.concatenate([values[:256, :64], values[512:, 64:]], axis=1)
    return np.concatenate(
        [np.concatenate(split_table(part, 2), axis=1) for part in (outer, values[256:512])], axis=0
    )


def dft_table():
    sample = np.arange(NT // 2)[:, None]
    tables = []
    for bins in (BIN_ORDER[: NBINS // 2], BIN_ORDER[NBINS // 2 :]):
        angle = (sample * bins[None, :] % NT) * (2.0 * np.pi / NT)
        table = np.concatenate([np.cos(angle), -np.sin(angle)], axis=1)
        tables.append(np.stack(split_table(table, 3)))
    return np.stack(tables)


def smooth_table():
    return (np.abs(BIN_ORDER[:, None] - BIN_ORDER[None, :]) <= 32).astype(BF16)


def lag_table():
    lags = (np.arange(LAGS) - LAGS // 2)[:, None]
    angle = (BIN_ORDER[None, :] * lags % NT) * (2.0 * np.pi / NT)
    groups = (LAGS, NBINS // 16, 16)
    table = np.stack([np.cos(angle).reshape(groups), -np.sin(angle).reshape(groups)], axis=2)
    return (table.reshape(LAGS, 2 * NBINS) / np.sqrt(SEG * NBINS)).astype(np.float32).astype(BF16)


def split_rows(value, terms):
    parts = []
    for term in range(terms):
        part = value.astype(BF16)
        parts.append(part)
        if term < terms - 1:
            value = value - part.astype(F32)
    return parts


def whiten_kernel(
    base_ref, x_hbm, fir_hbm, dft_hbm, smooth_hbm, dead_ref, out_hbm,
    x_ref, fir_ref, dft_ref, smooth_ref, seg_ref, turned_ref, sems,
):
    copies = [pltpu.make_async_copy(fir_hbm, fir_ref, sems.at[0])]
    for piece in range(4):
        lanes = pl.ds(PIECES[piece], PIECES[piece + 1] - PIECES[piece])
        copies.append(
            pltpu.make_async_copy(x_hbm.at[:, lanes], x_ref.at[:, lanes], sems.at[1 + piece])
        )
    copies.append(pltpu.make_async_copy(dft_hbm, dft_ref, sems.at[5]))
    copies.append(pltpu.make_async_copy(smooth_hbm, smooth_ref, sems.at[6]))
    for copy in copies:
        copy.start()
    copies[0].wait()
    edge = jnp.zeros((OWN, 128), F32)
    left_lanes = lax.broadcasted_iota(jnp.int32, (16 * OWN, 128), 1) < 64

    def filtered(parts, first, blocks, table):
        count = blocks * OWN
        windows = jnp.concatenate(
            [part[:, first + 512 * b : first + 512 * b + 256] for part in parts for b in range(blocks)],
            axis=0,
        )
        product = jnp.dot(windows, table, preferred_element_type=F32)
        return product[:count, :128] + (
            product[:count, 128:]
            + (
                product[count : 2 * count, :128]
                + (product[count : 2 * count, 128:] + product[2 * count :, :128])
            )
        )

    for piece in range(4):
        copies[1 + piece].wait()
        rows = x_ref[:, max(8192 * piece - 128, 0) : min(8192 * piece + 8320, 32768)]
        if piece == 0:
            rows = jnp.concatenate([edge, rows], axis=1)
        if piece == 3:
            rows = jnp.concatenate([rows, edge], axis=1)
        parts = split_rows(rows, 3)
        outer = filtered(parts, 0, 17, fir_ref[0:256])
        inner = filtered(parts, 256, 16, fir_ref[256:512])
        decimated = inner + jnp.where(left_lanes, outer[: 16 * OWN], outer[OWN:])
        for b in range(16):
            segment, part = 2 * piece + b // 8, b % 8
            seg_ref[segment * OWN : (segment + 1) * OWN, part * 128 : (part + 1) * 128] = (
                decimated[b * OWN : (b + 1) * OWN]
            )
    copies[5].wait()
    copies[6].wait()
    rows = SEG * OWN
    first, second = seg_ref[:, : NT // 2], seg_ref[:, NT // 2 :]
    halves = []
    for parity, folded in enumerate((first + second, first - second)):
        terms = jnp.concatenate(split_rows(folded, 3), axis=0)
        high = jnp.dot(terms, dft_ref[parity, 0], preferred_element_type=F32)
        mid = jnp.dot(terms[: 2 * rows], dft_ref[parity, 1], preferred_element_type=F32)
        low = jnp.dot(terms[:rows], dft_ref[parity, 2], preferred_element_type=F32)
        halves.append(
            high[:rows] + (high[rows : 2 * rows] + mid[:rows] + (high[2 * rows :] + mid[rows:] + low))
        )
    cut = NBINS // 2
    real_part = jnp.concatenate([halves[0][:, :cut], halves[1][:, :cut]], axis=1)
    imag_part = jnp.concatenate([halves[0][:, cut:], halves[1][:, cut:]], axis=1)
    power = real_part * real_part + imag_part * imag_part
    sums = jnp.dot(
        jnp.concatenate(split_rows(power, 2), axis=0), smooth_ref[...], preferred_element_type=F32
    )
    level = (sums[:rows] + sums[rows:]) / 65.0
    own_ids = base_ref[0] + (lax.broadcasted_iota(jnp.int32, (rows, 32), 0) & (OWN - 1))
    dead = jnp.max(jnp.where(dead_ref[...] == own_ids, 1.0, 0.0), axis=1, keepdims=True)
    scale = lax.rsqrt(level + 1e-06) * (1.0 - dead)
    real_part = real_part * scale
    imag_part = imag_part * scale
    chunk = lax.broadcasted_iota(jnp.int32, (OWN, 128), 1) >> 4
    sends = []
    for col in range(NBINS // 128):
        lanes = slice(col * 128, (col + 1) * 128)
        for kind, part in enumerate((real_part, imag_part)):
            tiles = [part[s * OWN : (s + 1) * OWN, lanes] for s in range(SEG)]
            for step in (1, 2, 4):
                low = (chunk & step) == 0
                for s in range(SEG):
                    if s & step == 0:
                        upper, lower = tiles[s], tiles[s + step]
                        tiles[s] = jnp.where(low, upper, pltpu.roll(lower, 16 * step, 1))
                        tiles[s + step] = jnp.where(low, pltpu.roll(upper, 128 - 16 * step, 1), lower)
            for member in range(SEG):
                first = (col * SEG + member) * 256 + kind * 128
                turned_ref[:, first : first + 128] = tiles[member].astype(BF16)
        wide = pl.ds(col * 2048, 2048)
        for copy in range(GROUP):
            send = pltpu.make_async_copy(
                turned_ref.at[:, wide], out_hbm.at[copy, :, wide], sems.at[7 + col * GROUP + copy]
            )
            send.start()
            sends.append(send)
    for send in sends:
        send.wait()


def pick_kernel(place_ref, sources_ref, line_ref, out_ref, wide_ref):
    for tile in range(WIDE // 128):
        first = tile // 4 * PITCH
        wide_ref[tile % 4, first : first + LINE] = line_ref[
            :, tile * 128 : (tile + 1) * 128
        ].astype(F32)
    for spot in range(PLANE):
        side, core, block = spot // 16, spot // 8 % 2, spot % 8
        index = 4 * ((block // 4) * 16 + (block % 4) * 4 + place_ref[0]) + core * 2 + side
        channel = sources_ref[index] & (LINE - 1)
        for col in range(4):
            rows = wide_ref[col, pl.ds(channel, 16, stride=PITCH), :]
            out_ref[spot, :, col * 128 : (col + 1) * 128] = rows.astype(BF16)


def hold_kernel(slot_ref, sources_ref, arrived_ref, out_ref):
    held = arrived_ref[sources_ref[slot_ref[0]] >> 6]
    for spot in range(SLOTS):
        out_ref[spot] = held


def corr_kernel(source_ref, own_ref, sibling_ref, lag_ref, out_ref, src_ref, cross_ref):
    src_ref[...] = source_ref[...].astype(F32)
    row = lax.broadcasted_iota(jnp.int32, (16, 256), 0)
    lane = lax.broadcasted_iota(jnp.int32, (16, 256), 1)
    real_mask = jnp.where(row == (lane & 15), 1.0, 0.0)
    imag_mask = jnp.where(lane < 128, real_mask, -real_mask)

    def group_step(line_row, side):
        group = line_row * 2 + side
        spread = []
        for slot in range(SLOTS):
            values = src_ref[slot, line_row : line_row + 1, side * 256 : (side + 1) * 256]
            swapped = jnp.concatenate([values[:, 128:], values[:, :128]], axis=1)
            spread.append((real_mask * values).astype(BF16))
            spread.append((imag_mask * swapped).astype(BF16))
        lanes = slice(group * 256, (group + 1) * 256)
        cross = lax.dot_general(
            jnp.concatenate(spread, axis=0),
            jnp.concatenate([own_ref[:, lanes], sibling_ref[:, lanes]], axis=0),
            (((1,), (1,)), ((), ())),
            preferred_element_type=F32,
        ).astype(BF16)
        rows = slice(group * 32, (group + 1) * 32)
        for slot in range(SLOTS):
            cross_ref[rows, slot * 128 : (slot + 1) * 128] = cross[slot * 32 : (slot + 1) * 32]

    for line_row in range(16):
        for side in range(2):
            group_step(line_row, side)
    for side in range(2):
        lanes = slice(side * 1024, (side + 1) * 1024)
        result = jnp.dot(
            lag_ref[...], cross_ref[:, lanes], preferred_element_type=F32
        ).astype(BF16)
        for block in range(8):
            for part in range(4):
                out_ref[part, block, :, side * 128 : (side + 1) * 128] = result[
                    part * 64 : (part + 1) * 64, block * 128 : (block + 1) * 128
                ]


def spread_kernel(in_ref, out_ref):
    for core in range(2):
        for far in range(2):
            for pair in range(2):
                left = in_ref[0, core, far, 2 * pair].astype(F32)
                right = in_ref[0, core, far, 2 * pair + 1].astype(F32)
                for part in range(4):
                    side, half = part // 2, part % 2
                    lanes = slice(part * LINE, (part + 1) * LINE)
                    spot = (core ^ half) * 512 + far * 256 + pair * 128
                    out_ref[2 * core + side, :, spot : spot + 128] = jnp.concatenate(
                        [left[:, lanes], right[:, lanes]], axis=1
                    )


def vmem():
    return pl.BlockSpec(memory_space=pltpu.VMEM)


def smem():
    return pl.BlockSpec(memory_space=pltpu.SMEM)


def whole():
    return pl.BlockSpec(memory_space=pl.ANY)


SMALL = pltpu.CompilerParams(vmem_limit_bytes=12 * 1024 * 1024)
MEDIUM = pltpu.CompilerParams(vmem_limit_bytes=20 * 1024 * 1024)
FULL = pltpu.CompilerParams(vmem_limit_bytes=60 * 1024 * 1024)


def call_whiten(base, records, dead_list):
    return pl.pallas_call(
        whiten_kernel,
        out_shape=jax.ShapeDtypeStruct((GROUP, OWN, WIDE), BF16),
        in_specs=[smem(), whole(), whole(), whole(), whole(), vmem()],
        out_specs=whole(),
        scratch_shapes=[
            pltpu.VMEM((OWN, 32768), F32),
            pltpu.VMEM((512, 256), BF16),
            pltpu.VMEM((2, 3, NT // 2, NBINS), BF16),
            pltpu.VMEM((NBINS, NBINS), BF16),
            pltpu.VMEM((SEG * OWN, NT), F32),
            pltpu.VMEM((OWN, WIDE), BF16),
            pltpu.SemaphoreType.DMA((23,)),
        ],
        compiler_params=FULL,
        name="whiten",
    )(
        base,
        records,
        jnp.asarray(fir_table()),
        jnp.asarray(dft_table()),
        jnp.asarray(smooth_table()),
        dead_list.reshape(1, 32),
    )


def call_pick(place, sources, line):
    return pl.pallas_call(
        pick_kernel,
        out_shape=jax.ShapeDtypeStruct((PLANE, 2 * SEG, NBINS), BF16),
        in_specs=[smem(), smem(), vmem()],
        out_specs=vmem(),
        scratch_shapes=[pltpu.VMEM((4, 17 * LINE, 128), F32)],
        compiler_params=SMALL,
        name="pick",
    )(place, sources, line)


def call_hold(slot, sources, arrived):
    return pl.pallas_call(
        hold_kernel,
        out_shape=jax.ShapeDtypeStruct((SLOTS, 2 * SEG, NBINS), BF16),
        in_specs=[smem(), smem(), vmem()],
        out_specs=vmem(),
        compiler_params=SMALL,
        name="hold",
    )(slot, sources, arrived)


def call_corr(source_spectra, own, sibling):
    return pl.pallas_call(
        corr_kernel,
        out_shape=jax.ShapeDtypeStruct((4, 8, LAGS // 4, 4 * LINE), BF16),
        in_specs=[vmem(), vmem(), vmem(), vmem()],
        out_specs=vmem(),
        scratch_shapes=[
            pltpu.VMEM((SLOTS, 16, 512), F32),
            pltpu.VMEM((2 * NBINS, SLOTS * 2 * LINE), BF16),
        ],
        compiler_params=MEDIUM,
        name="correlate",
    )(source_spectra, own, sibling, jnp.asarray(lag_table()))


def call_spread(gathered):
    return pl.pallas_call(
        spread_kernel,
        grid=(2,),
        out_shape=jax.ShapeDtypeStruct((4, LAGS // 4, PLANE * LINE), F32),
        in_specs=[
            pl.BlockSpec((1, 2, 2, 4, LAGS // 4, 4 * LINE), lambda i: (i, 0, 0, 0, 0, 0))
        ],
        out_specs=pl.BlockSpec((4, LAGS // 4, 16 * LINE), lambda i: (0, 0, i)),
        compiler_params=SMALL,
        name="spread",
    )(gathered)


def shards(records, sources, dead_list):
    xl_pos = lax.axis_index("xl")
    core_pos = lax.axis_index("core")
    xh_pos = lax.axis_index("xh")
    z_pos = lax.axis_index("z")
    y_pos = lax.axis_index("y")
    chan_pos = (xh_pos * 4 + z_pos) * 4 + y_pos
    device = (xl_pos * 2 + core_pos) * 32 + chan_pos
    own_slot = 4 * chan_pos + core_pos * 2 + xl_pos
    whitened = call_whiten((device * OWN).reshape(1), records, dead_list)
    line = lax.all_to_all(whitened, "y", 0, 0, tiled=True).reshape(LINE, WIDE)
    picked = call_pick(y_pos.reshape(1), sources, line)
    arrived = lax.all_to_all(picked, PLANE_AXES, 0, 0, tiled=True)
    arrived, sent_line = lax.optimization_barrier((arrived, line))
    sibling_line = lax.ppermute(sent_line, "core", [(0, 1), (1, 0)])
    held = call_hold(own_slot.reshape(1), sources, arrived)
    source_spectra = lax.all_to_all(held, SIDE_AXES, 0, 0, tiled=True)
    blocks = call_corr(source_spectra, sent_line, sibling_line)
    gathered = lax.all_to_all(
        blocks.reshape(PLANE, LAGS // 4, 4 * LINE), PLANE_AXES, 0, 0, tiled=True
    )
    return call_spread(gathered.reshape(2, 2, 2, 4, LAGS // 4, 4 * LINE))


def solution(mesh):
    inner = Mesh(mesh.devices.reshape(2, 2, 2, 4, 4), AXES)
    return jax.shard_map(
        shards,
        mesh=inner,
        in_specs=(P(AXES, None), P(), P()),
        out_specs=P(("xh", "z", "y"), ("xl", "core"), None),
        check_vma=False,
    )
```

```python
import numpy as np
import jax
import jax.numpy as jnp
from jax import lax
from jax.experimental import pallas as pl
from jax.experimental.pallas import tpu as pltpu
from jax.sharding import Mesh, PartitionSpec as P

NT = 1024
LAGS = 256
SEG = 8
NBINS = 512
OWN = 16
GROUP = 4
PLANE = 32
LINE = GROUP * OWN
AXES = ("xl", "core", "xh", "z", "y")
PLANE_AXES = ("xl", "core", "xh", "z")
SIDE_AXES = ("xl", "xh", "z")
SLOTS = 16
WIDE = 2 * SEG * NBINS
PITCH = LINE + 1
BIN_ORDER = np.concatenate([np.arange(4, 513, 4), np.arange(2, 512, 4), np.arange(1, 512, 2)])
PIECES = (0, 8320, 16512, 24704, 32768)
F32 = jnp.float32
BF16 = jnp.bfloat16


def split_table(table, terms):
    left = table.astype(np.float64)
    parts = []
    for _ in range(terms):
        part = left.astype(np.float32).astype(BF16)
        parts.append(part)
        left = left - part.astype(np.float64)
    return parts


def fir_table():
    row = np.arange(768)[:, None]
    col = np.arange(128)[None, :]
    offset = 4 * col + 255 - row
    inside = (offset >= 0) & (offset <= 254)
    tap = offset.astype(np.float64)
    hamming = 0.54 - 0.46 * np.cos(2.0 * np.pi * tap / 254.0)
    values = np.where(inside, 0.2 * np.sinc(0.2 * (tap - 127.0)) * hamming, 0.0)
    outer = np.concatenate([values[:256, :64], values[512:, 64:]], axis=1)
    return np.concatenate(
        [np.concatenate(split_table(part, 2), axis=1) for part in (outer, values[256:512])], axis=0
    )


def dft_table(samples, bins):
    angle = (np.arange(samples)[:, None] * bins[None, :] % NT) * (2.0 * np.pi / NT)
    return np.stack(split_table(np.concatenate([np.cos(angle), -np.sin(angle)], axis=1), 3))


def even_table():
    return np.stack([dft_table(256, BIN_ORDER[:128]), dft_table(256, BIN_ORDER[128:256])])


def odd_table():
    return dft_table(512, BIN_ORDER[256:])


def smooth_table():
    return (np.abs(BIN_ORDER[:, None] - BIN_ORDER[None, :]) <= 32).astype(BF16)


def lag_table():
    lags = (np.arange(LAGS) - LAGS // 2)[:, None]
    angle = (BIN_ORDER[None, :] * lags % NT) * (2.0 * np.pi / NT)
    groups = (LAGS, NBINS // 16, 16)
    table = np.stack([np.cos(angle).reshape(groups), -np.sin(angle).reshape(groups)], axis=2)
    return (table.reshape(LAGS, 2 * NBINS) / np.sqrt(SEG * NBINS)).astype(np.float32).astype(BF16)


def split_rows(value, terms):
    parts = []
    for term in range(terms):
        part = value.astype(BF16)
        parts.append(part)
        if term < terms - 1:
            value = value - part.astype(F32)
    return parts


def whiten_kernel(
    base_ref, x_hbm, fir_hbm, even_hbm, odd_hbm, smooth_hbm, dead_ref, out_hbm,
    x_ref, fir_ref, even_ref, odd_ref, smooth_ref, seg_ref, turned_ref, sems,
):
    copies = [pltpu.make_async_copy(fir_hbm, fir_ref, sems.at[0])]
    for piece in range(4):
        lanes = pl.ds(PIECES[piece], PIECES[piece + 1] - PIECES[piece])
        copies.append(
            pltpu.make_async_copy(x_hbm.at[:, lanes], x_ref.at[:, lanes], sems.at[1 + piece])
        )
    copies.append(pltpu.make_async_copy(even_hbm, even_ref, sems.at[5]))
    copies.append(pltpu.make_async_copy(odd_hbm, odd_ref, sems.at[6]))
    copies.append(pltpu.make_async_copy(smooth_hbm, smooth_ref, sems.at[7]))
    for copy in copies:
        copy.start()
    copies[0].wait()
    edge = jnp.zeros((OWN, 128), F32)
    left_lanes = lax.broadcasted_iota(jnp.int32, (16 * OWN, 128), 1) < 64

    def filtered(parts, first, blocks, table):
        count = blocks * OWN
        windows = jnp.concatenate(
            [part[:, first + 512 * b : first + 512 * b + 256] for part in parts for b in range(blocks)],
            axis=0,
        )
        product = jnp.dot(windows, table, preferred_element_type=F32)
        return product[:count, :128] + (
            product[:count, 128:]
            + (
                product[count : 2 * count, :128]
                + (product[count : 2 * count, 128:] + product[2 * count :, :128])
            )
        )

    for piece in range(4):
        copies[1 + piece].wait()
        rows = x_ref[:, max(8192 * piece - 128, 0) : min(8192 * piece + 8320, 32768)]
        if piece == 0:
            rows = jnp.concatenate([edge, rows], axis=1)
        if piece == 3:
            rows = jnp.concatenate([rows, edge], axis=1)
        parts = split_rows(rows, 3)
        outer = filtered(parts, 0, 17, fir_ref[0:256])
        inner = filtered(parts, 256, 16, fir_ref[256:512])
        decimated = inner + jnp.where(left_lanes, outer[: 16 * OWN], outer[OWN:])
        for b in range(16):
            segment, part = 2 * piece + b // 8, b % 8
            seg_ref[segment * OWN : (segment + 1) * OWN, part * 128 : (part + 1) * 128] = (
                decimated[b * OWN : (b + 1) * OWN]
            )
    for copy in copies[5:]:
        copy.wait()
    rows = SEG * OWN

    def transform(folded, table_ref):
        terms = jnp.concatenate(split_rows(folded, 3), axis=0)
        high = jnp.dot(terms, table_ref[0], preferred_element_type=F32)
        mid = jnp.dot(terms[: 2 * rows], table_ref[1], preferred_element_type=F32)
        low = jnp.dot(terms[:rows], table_ref[2], preferred_element_type=F32)
        return high[:rows] + (
            high[rows : 2 * rows] + mid[:rows] + (high[2 * rows :] + mid[rows:] + low)
        )

    first, second = seg_ref[:, : NT // 2], seg_ref[:, NT // 2 :]
    even, odd = first + second, first - second
    first, second = even[:, : NT // 4], even[:, NT // 4 :]
    fours = transform(first + second, even_ref.at[0])
    twos = transform(first - second, even_ref.at[1])
    odds = transform(odd, odd_ref)
    real_part = jnp.concatenate([fours[:, :128], twos[:, :128], odds[:, :256]], axis=1)
    imag_part = jnp.concatenate([fours[:, 128:], twos[:, 128:], odds[:, 256:]], axis=1)
    power = real_part * real_part + imag_part * imag_part
    sums = jnp.dot(
        jnp.concatenate(split_rows(power, 2), axis=0), smooth_ref[...], preferred_element_type=F32
    )
    level = (sums[:rows] + sums[rows:]) / 65.0
    own_ids = base_ref[0] + (lax.broadcasted_iota(jnp.int32, (rows, 32), 0) & (OWN - 1))
    dead = jnp.max(jnp.where(dead_ref[...] == own_ids, 1.0, 0.0), axis=1, keepdims=True)
    scale = lax.rsqrt(level + 1e-06) * (1.0 - dead)
    real_part = real_part * scale
    imag_part = imag_part * scale
    chunk = lax.broadcasted_iota(jnp.int32, (OWN, 128), 1) >> 4
    sends = []
    for col in range(NBINS // 128):
        lanes = slice(col * 128, (col + 1) * 128)
        for kind, part in enumerate((real_part, imag_part)):
            tiles = [part[s * OWN : (s + 1) * OWN, lanes] for s in range(SEG)]
            for step in (1, 2, 4):
                low = (chunk & step) == 0
                for s in range(SEG):
                    if s & step == 0:
                        upper, lower = tiles[s], tiles[s + step]
                        tiles[s] = jnp.where(low, upper, pltpu.roll(lower, 16 * step, 1))
                        tiles[s + step] = jnp.where(low, pltpu.roll(upper, 128 - 16 * step, 1), lower)
            for member in range(SEG):
                first = (col * SEG + member) * 256 + kind * 128
                turned_ref[:, first : first + 128] = tiles[member].astype(BF16)
        wide = pl.ds(col * 2048, 2048)
        for copy in range(GROUP):
            send = pltpu.make_async_copy(
                turned_ref.at[:, wide], out_hbm.at[copy, :, wide], sems.at[8 + col * GROUP + copy]
            )
            send.start()
            sends.append(send)
    for send in sends:
        send.wait()


def pick_kernel(place_ref, sources_ref, line_ref, out_ref, wide_ref):
    for tile in range(WIDE // 128):
        first = tile // 4 * PITCH
        wide_ref[tile % 4, first : first + LINE] = line_ref[
            :, tile * 128 : (tile + 1) * 128
        ].astype(F32)
    for spot in range(PLANE):
        side, core, block = spot // 16, spot // 8 % 2, spot % 8
        index = 4 * ((block // 4) * 16 + (block % 4) * 4 + place_ref[0]) + core * 2 + side
        channel = sources_ref[index] & (LINE - 1)
        for col in range(4):
            rows = wide_ref[col, pl.ds(channel, 16, stride=PITCH), :]
            out_ref[spot, :, col * 128 : (col + 1) * 128] = rows.astype(BF16)


def hold_kernel(slot_ref, sources_ref, arrived_ref, out_ref):
    held = arrived_ref[sources_ref[slot_ref[0]] >> 6]
    for spot in range(SLOTS):
        out_ref[spot] = held


def corr_kernel(source_ref, own_ref, sibling_ref, lag_ref, out_ref, src_ref, cross_ref):
    src_ref[...] = source_ref[...].astype(F32)
    row = lax.broadcasted_iota(jnp.int32, (16, 256), 0)
    lane = lax.broadcasted_iota(jnp.int32, (16, 256), 1)
    real_mask = jnp.where(row == (lane & 15), 1.0, 0.0)
    imag_mask = jnp.where(lane < 128, real_mask, -real_mask)

    def group_step(line_row, side):
        group = line_row * 2 + side
        spread = []
        for slot in range(SLOTS):
            values = src_ref[slot, line_row : line_row + 1, side * 256 : (side + 1) * 256]
            swapped = jnp.concatenate([values[:, 128:], values[:, :128]], axis=1)
            spread.append((real_mask * values).astype(BF16))
            spread.append((imag_mask * swapped).astype(BF16))
        lanes = slice(group * 256, (group + 1) * 256)
        cross = lax.dot_general(
            jnp.concatenate(spread, axis=0),
            jnp.concatenate([own_ref[:, lanes], sibling_ref[:, lanes]], axis=0),
            (((1,), (1,)), ((), ())),
            preferred_element_type=F32,
        ).astype(BF16)
        rows = slice(group * 32, (group + 1) * 32)
        for slot in range(SLOTS):
            cross_ref[rows, slot * 128 : (slot + 1) * 128] = cross[slot * 32 : (slot + 1) * 32]

    for line_row in range(16):
        for side in range(2):
            group_step(line_row, side)
    for side in range(2):
        lanes = slice(side * 1024, (side + 1) * 1024)
        result = jnp.dot(
            lag_ref[...], cross_ref[:, lanes], preferred_element_type=F32
        ).astype(BF16)
        for block in range(8):
            for part in range(4):
                out_ref[part, block, :, side * 128 : (side + 1) * 128] = result[
                    part * 64 : (part + 1) * 64, block * 128 : (block + 1) * 128
                ]


def spread_kernel(in_ref, out_hbm, wide_ref, sems):
    sends = []
    for far_side in range(2):
        for core in range(2):
            for far in range(2):
                for pair in range(2):
                    left = in_ref[far_side, core, far, 2 * pair].astype(F32)
                    right = in_ref[far_side, core, far, 2 * pair + 1].astype(F32)
                    for part in range(4):
                        side, half = part // 2, part % 2
                        lanes = slice(part * LINE, (part + 1) * LINE)
                        spot = far_side * 1024 + (core ^ half) * 512 + far * 256 + pair * 128
                        wide_ref[2 * core + side, :, spot : spot + 128] = jnp.concatenate(
                            [left[:, lanes], right[:, lanes]], axis=1
                        )
            for side in range(2):
                spot = pl.ds(far_side * 1024, 1024)
                send = pltpu.make_async_copy(
                    wide_ref.at[2 * core + side, :, spot],
                    out_hbm.at[2 * core + side, :, spot],
                    sems.at[len(sends)],
                )
                send.start()
                sends.append(send)
    for send in sends:
        send.wait()


def vmem():
    return pl.BlockSpec(memory_space=pltpu.VMEM)


def smem():
    return pl.BlockSpec(memory_space=pltpu.SMEM)


def whole():
    return pl.BlockSpec(memory_space=pl.ANY)


SMALL = pltpu.CompilerParams(vmem_limit_bytes=12 * 1024 * 1024)
MEDIUM = pltpu.CompilerParams(vmem_limit_bytes=20 * 1024 * 1024)
FULL = pltpu.CompilerParams(vmem_limit_bytes=60 * 1024 * 1024)


def call_whiten(base, records, dead_list):
    return pl.pallas_call(
        whiten_kernel,
        out_shape=jax.ShapeDtypeStruct((GROUP, OWN, WIDE), BF16),
        in_specs=[smem(), whole(), whole(), whole(), whole(), whole(), vmem()],
        out_specs=whole(),
        scratch_shapes=[
            pltpu.VMEM((OWN, 32768), F32),
            pltpu.VMEM((512, 256), BF16),
            pltpu.VMEM((2, 3, NT // 4, NBINS // 2), BF16),
            pltpu.VMEM((3, NT // 2, NBINS), BF16),
            pltpu.VMEM((NBINS, NBINS), BF16),
            pltpu.VMEM((SEG * OWN, NT), F32),
            pltpu.VMEM((OWN, WIDE), BF16),
            pltpu.SemaphoreType.DMA((24,)),
        ],
        compiler_params=FULL,
        name="whiten",
    )(
        base,
        records,
        jnp.asarray(fir_table()),
        jnp.asarray(even_table()),
        jnp.asarray(odd_table()),
        jnp.asarray(smooth_table()),
        dead_list.reshape(1, 32),
    )


def call_pick(place, sources, line):
    return pl.pallas_call(
        pick_kernel,
        out_shape=jax.ShapeDtypeStruct((PLANE, 2 * SEG, NBINS), BF16),
        in_specs=[smem(), smem(), vmem()],
        out_specs=vmem(),
        scratch_shapes=[pltpu.VMEM((4, 17 * LINE, 128), F32)],
        compiler_params=SMALL,
        name="pick",
    )(place, sources, line)


def call_hold(slot, sources, arrived):
    return pl.pallas_call(
        hold_kernel,
        out_shape=jax.ShapeDtypeStruct((SLOTS, 2 * SEG, NBINS), BF16),
        in_specs=[smem(), smem(), vmem()],
        out_specs=vmem(),
        compiler_params=SMALL,
        name="hold",
    )(slot, sources, arrived)


def call_corr(source_spectra, own, sibling):
    return pl.pallas_call(
        corr_kernel,
        out_shape=jax.ShapeDtypeStruct((4, 8, LAGS // 4, 4 * LINE), BF16),
        in_specs=[vmem(), vmem(), vmem(), vmem()],
        out_specs=vmem(),
        scratch_shapes=[
            pltpu.VMEM((SLOTS, 16, 512), F32),
            pltpu.VMEM((2 * NBINS, SLOTS * 2 * LINE), BF16),
        ],
        compiler_params=MEDIUM,
        name="correlate",
    )(source_spectra, own, sibling, jnp.asarray(lag_table()))


def call_spread(gathered):
    return pl.pallas_call(
        spread_kernel,
        out_shape=jax.ShapeDtypeStruct((4, LAGS // 4, PLANE * LINE), F32),
        in_specs=[vmem()],
        out_specs=whole(),
        scratch_shapes=[
            pltpu.VMEM((4, LAGS // 4, PLANE * LINE), F32),
            pltpu.SemaphoreType.DMA((8,)),
        ],
        compiler_params=SMALL,
        name="spread",
    )(gathered)


def shards(records, sources, dead_list):
    xl_pos = lax.axis_index("xl")
    core_pos = lax.axis_index("core")
    xh_pos = lax.axis_index("xh")
    z_pos = lax.axis_index("z")
    y_pos = lax.axis_index("y")
    chan_pos = (xh_pos * 4 + z_pos) * 4 + y_pos
    device = (xl_pos * 2 + core_pos) * 32 + chan_pos
    own_slot = 4 * chan_pos + core_pos * 2 + xl_pos
    whitened = call_whiten((device * OWN).reshape(1), records, dead_list)
    line = lax.all_to_all(whitened, "y", 0, 0, tiled=True).reshape(LINE, WIDE)
    picked = call_pick(y_pos.reshape(1), sources, line)
    arrived = lax.all_to_all(picked, PLANE_AXES, 0, 0, tiled=True)
    arrived, sent_line = lax.optimization_barrier((arrived, line))
    sibling_line = lax.ppermute(sent_line, "core", [(0, 1), (1, 0)])
    held = call_hold(own_slot.reshape(1), sources, arrived)
    source_spectra = lax.all_to_all(held, SIDE_AXES, 0, 0, tiled=True)
    blocks = call_corr(source_spectra, sent_line, sibling_line)
    gathered = lax.all_to_all(
        blocks.reshape(PLANE, LAGS // 4, 4 * LINE), PLANE_AXES, 0, 0, tiled=True
    )
    return call_spread(gathered.reshape(2, 2, 2, 4, LAGS // 4, 4 * LINE))


def solution(mesh):
    inner = Mesh(mesh.devices.reshape(2, 2, 2, 4, 4), AXES)
    return jax.shard_map(
        shards,
        mesh=inner,
        in_specs=(P(AXES, None), P(), P()),
        out_specs=P(("xh", "z", "y"), ("xl", "core"), None),
        check_vma=False,
    )
```

```python
import numpy as np
import jax
import jax.numpy as jnp
from jax import lax
from jax.experimental import pallas as pl
from jax.experimental.pallas import tpu as pltpu
from jax.sharding import Mesh, PartitionSpec as P

NT = 1024
LAGS = 256
SEG = 8
NBINS = 512
OWN = 16
GROUP = 4
PLANE = 32
LINE = GROUP * OWN
AXES = ("xl", "core", "xh", "z", "y")
PLANE_AXES = ("xl", "core", "xh", "z")
SIDE_AXES = ("xl", "xh", "z")
SLOTS = 16
WIDE = 2 * SEG * NBINS
PITCH = LINE + 1
BIN_ORDER = np.concatenate([np.arange(4, 513, 4), np.arange(2, 512, 4), np.arange(1, 512, 2)])
PIECES = (0, 8320, 16512, 24704, 32768)
F32 = jnp.float32
BF16 = jnp.bfloat16


def split_table(table, terms):
    left = table.astype(np.float64)
    parts = []
    for _ in range(terms):
        part = left.astype(np.float32).astype(BF16)
        parts.append(part)
        left = left - part.astype(np.float64)
    return parts


def fir_table():
    row = np.arange(768)[:, None]
    col = np.arange(128)[None, :]
    offset = 4 * col + 255 - row
    inside = (offset >= 0) & (offset <= 254)
    tap = offset.astype(np.float64)
    hamming = 0.54 - 0.46 * np.cos(2.0 * np.pi * tap / 254.0)
    values = np.where(inside, 0.2 * np.sinc(0.2 * (tap - 127.0)) * hamming, 0.0)
    outer = np.concatenate([values[:256, :64], values[512:, 64:]], axis=1)
    return np.concatenate(
        [np.concatenate(split_table(part, 2), axis=1) for part in (outer, values[256:512])], axis=0
    )


def dft_table(samples, bins):
    angle = (np.arange(samples)[:, None] * bins[None, :] % NT) * (2.0 * np.pi / NT)
    return np.stack(split_table(np.concatenate([np.cos(angle), -np.sin(angle)], axis=1), 3))


def even_table():
    return np.stack([dft_table(256, BIN_ORDER[:128]), dft_table(256, BIN_ORDER[128:256])])


def odd_table():
    return dft_table(512, BIN_ORDER[256:])


def smooth_table():
    return (np.abs(BIN_ORDER[:, None] - BIN_ORDER[None, :]) <= 32).astype(BF16)


def lag_table():
    lags = (np.arange(LAGS) - LAGS // 2)[:, None]
    angle = (BIN_ORDER[None, :] * lags % NT) * (2.0 * np.pi / NT)
    groups = (LAGS, NBINS // 16, 16)
    table = np.stack([np.cos(angle).reshape(groups), -np.sin(angle).reshape(groups)], axis=2)
    return (table.reshape(LAGS, 2 * NBINS) / np.sqrt(SEG * NBINS)).astype(np.float32).astype(BF16)


def split_rows(value, terms):
    parts = []
    for term in range(terms):
        part = value.astype(BF16)
        parts.append(part)
        if term < terms - 1:
            value = value - part.astype(F32)
    return parts


def whiten_kernel(
    base_ref, x_hbm, fir_hbm, even_hbm, odd_hbm, smooth_hbm, dead_ref, out_hbm,
    x_ref, fir_ref, even_ref, odd_ref, smooth_ref, seg_ref, turned_ref, sems,
):
    copies = [pltpu.make_async_copy(fir_hbm, fir_ref, sems.at[0])]
    for piece in range(4):
        lanes = pl.ds(PIECES[piece], PIECES[piece + 1] - PIECES[piece])
        copies.append(
            pltpu.make_async_copy(x_hbm.at[:, lanes], x_ref.at[:, lanes], sems.at[1 + piece])
        )
    copies.append(pltpu.make_async_copy(even_hbm, even_ref, sems.at[5]))
    copies.append(pltpu.make_async_copy(odd_hbm, odd_ref, sems.at[6]))
    copies.append(pltpu.make_async_copy(smooth_hbm, smooth_ref, sems.at[7]))
    for copy in copies:
        copy.start()
    copies[0].wait()
    edge = jnp.zeros((OWN, 128), F32)
    left_lanes = lax.broadcasted_iota(jnp.int32, (16 * OWN, 128), 1) < 64

    def filtered(parts, first, blocks, table):
        count = blocks * OWN
        windows = jnp.concatenate(
            [part[:, first + 512 * b : first + 512 * b + 256] for part in parts for b in range(blocks)],
            axis=0,
        )
        product = jnp.dot(windows, table, preferred_element_type=F32)
        return product[:count, :128] + (
            product[:count, 128:]
            + (
                product[count : 2 * count, :128]
                + (product[count : 2 * count, 128:] + product[2 * count :, :128])
            )
        )

    for piece in range(4):
        copies[1 + piece].wait()
        rows = x_ref[:, max(8192 * piece - 128, 0) : min(8192 * piece + 8320, 32768)]
        if piece == 0:
            rows = jnp.concatenate([edge, rows], axis=1)
        if piece == 3:
            rows = jnp.concatenate([rows, edge], axis=1)
        parts = split_rows(rows, 3)
        outer = filtered(parts, 0, 17, fir_ref[0:256])
        inner = filtered(parts, 256, 16, fir_ref[256:512])
        decimated = inner + jnp.where(left_lanes, outer[: 16 * OWN], outer[OWN:])
        for b in range(16):
            segment, part = 2 * piece + b // 8, b % 8
            seg_ref[segment * OWN : (segment + 1) * OWN, part * 128 : (part + 1) * 128] = (
                decimated[b * OWN : (b + 1) * OWN]
            )
    for copy in copies[5:]:
        copy.wait()
    rows = SEG * OWN

    def transform(folded, table_ref):
        terms = jnp.concatenate(split_rows(folded, 3), axis=0)
        high = jnp.dot(terms, table_ref[0], preferred_element_type=F32)
        mid = jnp.dot(terms[: 2 * rows], table_ref[1], preferred_element_type=F32)
        low = jnp.dot(terms[:rows], table_ref[2], preferred_element_type=F32)
        return high[:rows] + (
            high[rows : 2 * rows] + mid[:rows] + (high[2 * rows :] + mid[rows:] + low)
        )

    first, second = seg_ref[:, : NT // 2], seg_ref[:, NT // 2 :]
    even, odd = first + second, first - second
    first, second = even[:, : NT // 4], even[:, NT // 4 :]
    fours = transform(first + second, even_ref.at[0])
    twos = transform(first - second, even_ref.at[1])
    odds = transform(odd, odd_ref)
    real_part = jnp.concatenate([fours[:, :128], twos[:, :128], odds[:, :256]], axis=1)
    imag_part = jnp.concatenate([fours[:, 128:], twos[:, 128:], odds[:, 256:]], axis=1)
    power = real_part * real_part + imag_part * imag_part
    sums = jnp.dot(
        jnp.concatenate(split_rows(power, 2), axis=0), smooth_ref[...], preferred_element_type=F32
    )
    level = (sums[:rows] + sums[rows:]) / 65.0
    own_ids = base_ref[0] + (lax.broadcasted_iota(jnp.int32, (rows, 32), 0) & (OWN - 1))
    dead = jnp.max(jnp.where(dead_ref[...] == own_ids, 1.0, 0.0), axis=1, keepdims=True)
    scale = lax.rsqrt(level + 1e-06) * (1.0 - dead)
    real_part = real_part * scale
    imag_part = imag_part * scale
    chunk = lax.broadcasted_iota(jnp.int32, (OWN, 128), 1) >> 4
    sends = []
    for col in range(NBINS // 128):
        lanes = slice(col * 128, (col + 1) * 128)
        for kind, part in enumerate((real_part, imag_part)):
            tiles = [part[s * OWN : (s + 1) * OWN, lanes] for s in range(SEG)]
            for step in (1, 2, 4):
                low = (chunk & step) == 0
                for s in range(SEG):
                    if s & step == 0:
                        upper, lower = tiles[s], tiles[s + step]
                        tiles[s] = jnp.where(low, upper, pltpu.roll(lower, 16 * step, 1))
                        tiles[s + step] = jnp.where(low, pltpu.roll(upper, 128 - 16 * step, 1), lower)
            for member in range(SEG):
                first = (col * SEG + member) * 256 + kind * 128
                turned_ref[:, first : first + 128] = tiles[member].astype(BF16)
        wide = pl.ds(col * 2048, 2048)
        send = pltpu.make_async_copy(
            turned_ref.at[:, wide], out_hbm.at[:, wide], sems.at[8 + col]
        )
        send.start()
        sends.append(send)
    for send in sends:
        send.wait()


def pick_kernel(place_ref, sources_ref, *refs):
    parts, (out_ref, line_ref, wide_ref) = refs[:GROUP], refs[GROUP:]
    for step, part_ref in enumerate(parts):
        spot = pl.multiple_of(((place_ref[0] + step) & 3) * OWN, OWN)
        line_ref[pl.ds(spot, OWN), :] = part_ref[...]
    for tile in range(WIDE // 128):
        lanes = slice(tile * 128, (tile + 1) * 128)
        rows = jnp.concatenate([part_ref[:, lanes].astype(F32) for part_ref in parts], axis=0)
        first = tile // 4 * PITCH
        wide_ref[tile % 4, first : first + LINE] = rows
    for spot in range(PLANE):
        side, core, block = spot // 16, spot // 8 % 2, spot % 8
        index = 4 * ((block // 4) * 16 + (block % 4) * 4 + place_ref[0]) + core * 2 + side
        source = sources_ref[index]
        channel = (((source >> 4) - place_ref[0]) & 3) * OWN + (source & (OWN - 1))
        for col in range(4):
            rows = wide_ref[col, pl.ds(channel, 16, stride=PITCH), :]
            out_ref[spot, :, col * 128 : (col + 1) * 128] = rows.astype(BF16)


def hold_kernel(slot_ref, sources_ref, arrived_ref, out_ref):
    held = arrived_ref[sources_ref[slot_ref[0]] >> 6]
    for spot in range(SLOTS):
        out_ref[spot] = held


def corr_kernel(source_ref, own_ref, sibling_ref, lag_ref, out_ref, src_ref, cross_ref):
    src_ref[...] = source_ref[...].astype(F32)
    row = lax.broadcasted_iota(jnp.int32, (16, 256), 0)
    lane = lax.broadcasted_iota(jnp.int32, (16, 256), 1)
    real_mask = jnp.where(row == (lane & 15), 1.0, 0.0)
    imag_mask = jnp.where(lane < 128, real_mask, -real_mask)

    def group_step(line_row, side):
        group = line_row * 2 + side
        spread = []
        for slot in range(SLOTS):
            values = src_ref[slot, line_row : line_row + 1, side * 256 : (side + 1) * 256]
            swapped = jnp.concatenate([values[:, 128:], values[:, :128]], axis=1)
            spread.append((real_mask * values).astype(BF16))
            spread.append((imag_mask * swapped).astype(BF16))
        lanes = slice(group * 256, (group + 1) * 256)
        cross = lax.dot_general(
            jnp.concatenate(spread, axis=0),
            jnp.concatenate([own_ref[:, lanes], sibling_ref[:, lanes]], axis=0),
            (((1,), (1,)), ((), ())),
            preferred_element_type=F32,
        ).astype(BF16)
        rows = slice(group * 32, (group + 1) * 32)
        for slot in range(SLOTS):
            cross_ref[rows, slot * 128 : (slot + 1) * 128] = cross[slot * 32 : (slot + 1) * 32]

    for line_row in range(16):
        for side in range(2):
            group_step(line_row, side)
    for side in range(2):
        lanes = slice(side * 1024, (side + 1) * 1024)
        result = jnp.dot(
            lag_ref[...], cross_ref[:, lanes], preferred_element_type=F32
        ).astype(BF16)
        for block in range(8):
            for part in range(4):
                out_ref[part, block, :, side * 128 : (side + 1) * 128] = result[
                    part * 64 : (part + 1) * 64, block * 128 : (block + 1) * 128
                ]


def spread_kernel(in_ref, out_hbm, wide_ref, sems):
    sends = []
    for far_side in range(2):
        for core in range(2):
            for far in range(2):
                for pair in range(2):
                    left = in_ref[far_side, core, far, 2 * pair].astype(F32)
                    right = in_ref[far_side, core, far, 2 * pair + 1].astype(F32)
                    for part in range(4):
                        side, half = part // 2, part % 2
                        lanes = slice(part * LINE, (part + 1) * LINE)
                        spot = far_side * 1024 + (core ^ half) * 512 + far * 256 + pair * 128
                        wide_ref[2 * core + side, :, spot : spot + 128] = jnp.concatenate(
                            [left[:, lanes], right[:, lanes]], axis=1
                        )
            for side in range(2):
                spot = pl.ds(far_side * 1024, 1024)
                send = pltpu.make_async_copy(
                    wide_ref.at[2 * core + side, :, spot],
                    out_hbm.at[2 * core + side, :, spot],
                    sems.at[len(sends)],
                )
                send.start()
                sends.append(send)
    for send in sends:
        send.wait()


def vmem():
    return pl.BlockSpec(memory_space=pltpu.VMEM)


def smem():
    return pl.BlockSpec(memory_space=pltpu.SMEM)


def whole():
    return pl.BlockSpec(memory_space=pl.ANY)


SMALL = pltpu.CompilerParams(vmem_limit_bytes=12 * 1024 * 1024)
MEDIUM = pltpu.CompilerParams(vmem_limit_bytes=20 * 1024 * 1024)
FULL = pltpu.CompilerParams(vmem_limit_bytes=60 * 1024 * 1024)


def call_whiten(base, records, dead_list):
    return pl.pallas_call(
        whiten_kernel,
        out_shape=jax.ShapeDtypeStruct((OWN, WIDE), BF16),
        in_specs=[smem(), whole(), whole(), whole(), whole(), whole(), vmem()],
        out_specs=whole(),
        scratch_shapes=[
            pltpu.VMEM((OWN, 32768), F32),
            pltpu.VMEM((512, 256), BF16),
            pltpu.VMEM((2, 3, NT // 4, NBINS // 2), BF16),
            pltpu.VMEM((3, NT // 2, NBINS), BF16),
            pltpu.VMEM((NBINS, NBINS), BF16),
            pltpu.VMEM((SEG * OWN, NT), F32),
            pltpu.VMEM((OWN, WIDE), BF16),
            pltpu.SemaphoreType.DMA((12,)),
        ],
        compiler_params=FULL,
        name="whiten",
    )(
        base,
        records,
        jnp.asarray(fir_table()),
        jnp.asarray(even_table()),
        jnp.asarray(odd_table()),
        jnp.asarray(smooth_table()),
        dead_list.reshape(1, 32),
    )


def call_pick(place, sources, parts):
    return pl.pallas_call(
        pick_kernel,
        out_shape=(
            jax.ShapeDtypeStruct((PLANE, 2 * SEG, NBINS), BF16),
            jax.ShapeDtypeStruct((LINE, WIDE), BF16),
        ),
        in_specs=[smem(), smem()] + [vmem()] * GROUP,
        out_specs=(vmem(), vmem()),
        scratch_shapes=[pltpu.VMEM((4, 17 * LINE, 128), F32)],
        compiler_params=SMALL,
        name="pick",
    )(place, sources, *parts)


def call_hold(slot, sources, arrived):
    return pl.pallas_call(
        hold_kernel,
        out_shape=jax.ShapeDtypeStruct((SLOTS, 2 * SEG, NBINS), BF16),
        in_specs=[smem(), smem(), vmem()],
        out_specs=vmem(),
        compiler_params=SMALL,
        name="hold",
    )(slot, sources, arrived)


def call_corr(source_spectra, own, sibling):
    return pl.pallas_call(
        corr_kernel,
        out_shape=jax.ShapeDtypeStruct((4, 8, LAGS // 4, 4 * LINE), BF16),
        in_specs=[vmem(), vmem(), vmem(), vmem()],
        out_specs=vmem(),
        scratch_shapes=[
            pltpu.VMEM((SLOTS, 16, 512), F32),
            pltpu.VMEM((2 * NBINS, SLOTS * 2 * LINE), BF16),
        ],
        compiler_params=MEDIUM,
        name="correlate",
    )(source_spectra, own, sibling, jnp.asarray(lag_table()))


def call_spread(gathered):
    return pl.pallas_call(
        spread_kernel,
        out_shape=jax.ShapeDtypeStruct((4, LAGS // 4, PLANE * LINE), F32),
        in_specs=[vmem()],
        out_specs=whole(),
        scratch_shapes=[
            pltpu.VMEM((4, LAGS // 4, PLANE * LINE), F32),
            pltpu.SemaphoreType.DMA((8,)),
        ],
        compiler_params=SMALL,
        name="spread",
    )(gathered)


def shards(records, sources, dead_list):
    xl_pos = lax.axis_index("xl")
    core_pos = lax.axis_index("core")
    xh_pos = lax.axis_index("xh")
    z_pos = lax.axis_index("z")
    y_pos = lax.axis_index("y")
    chan_pos = (xh_pos * 4 + z_pos) * 4 + y_pos
    device = (xl_pos * 2 + core_pos) * 32 + chan_pos
    own_slot = 4 * chan_pos + core_pos * 2 + xl_pos
    whitened = call_whiten((device * OWN).reshape(1), records, dead_list)
    parts = {0: whitened}
    for step in (2, 1, 3):
        parts[step] = lax.ppermute(whitened, "y", [(i, (i - step) % GROUP) for i in range(GROUP)])
    parts = [parts[step] for step in range(GROUP)]
    picked, line = call_pick(y_pos.reshape(1), sources, parts)
    arrived = lax.all_to_all(picked, PLANE_AXES, 0, 0, tiled=True)
    arrived, sent_line = lax.optimization_barrier((arrived, line))
    sibling_line = lax.ppermute(sent_line, "core", [(0, 1), (1, 0)])
    held = call_hold(own_slot.reshape(1), sources, arrived)
    source_spectra = lax.all_to_all(held, SIDE_AXES, 0, 0, tiled=True)
    blocks = call_corr(source_spectra, sent_line, sibling_line)
    gathered = lax.all_to_all(
        blocks.reshape(PLANE, LAGS // 4, 4 * LINE), PLANE_AXES, 0, 0, tiled=True
    )
    return call_spread(gathered.reshape(2, 2, 2, 4, LAGS // 4, 4 * LINE))


def solution(mesh):
    inner = Mesh(mesh.devices.reshape(2, 2, 2, 4, 4), AXES)
    return jax.shard_map(
        shards,
        mesh=inner,
        in_specs=(P(AXES, None), P(), P()),
        out_specs=P(("xh", "z", "y"), ("xl", "core"), None),
        check_vma=False,
    )
```

```python
import numpy as np
import jax
import jax.numpy as jnp
from jax import lax
from jax.experimental import pallas as pl
from jax.experimental.pallas import tpu as pltpu
from jax.sharding import Mesh, PartitionSpec as P

NT = 1024
LAGS = 256
SEG = 8
NBINS = 512
OWN = 16
GROUP = 4
PLANE = 32
LINE = GROUP * OWN
AXES = ("xl", "core", "xh", "z", "y")
PLANE_AXES = ("xl", "core", "xh", "z")
SIDE_AXES = ("xl", "xh", "z")
SLOTS = 16
WIDE = 2 * SEG * NBINS
PITCH = LINE + 1
BIN_ORDER = np.concatenate([np.arange(4, 513, 4), np.arange(2, 512, 4), np.arange(1, 512, 2)])
PIECES = (0, 8320, 16512, 24704, 32768)
F32 = jnp.float32
BF16 = jnp.bfloat16


def split_table(table, terms):
    left = table.astype(np.float64)
    parts = []
    for _ in range(terms):
        part = left.astype(np.float32).astype(BF16)
        parts.append(part)
        left = left - part.astype(np.float64)
    return parts


def fir_table():
    row = np.arange(768)[:, None]
    col = np.arange(128)[None, :]
    offset = 4 * col + 255 - row
    inside = (offset >= 0) & (offset <= 254)
    tap = offset.astype(np.float64)
    hamming = 0.54 - 0.46 * np.cos(2.0 * np.pi * tap / 254.0)
    values = np.where(inside, 0.2 * np.sinc(0.2 * (tap - 127.0)) * hamming, 0.0)
    outer = np.concatenate([values[:256, :64], values[512:, 64:]], axis=1)
    return np.concatenate(
        [np.concatenate(split_table(part, 2), axis=1) for part in (outer, values[256:512])], axis=0
    )


def dft_table(samples, bins):
    angle = (np.arange(samples)[:, None] * bins[None, :] % NT) * (2.0 * np.pi / NT)
    return np.stack(split_table(np.concatenate([np.cos(angle), -np.sin(angle)], axis=1), 3))


def even_table():
    return np.stack([dft_table(256, BIN_ORDER[:128]), dft_table(256, BIN_ORDER[128:256])])


def odd_table():
    return dft_table(512, BIN_ORDER[256:])


def smooth_table():
    return (np.abs(BIN_ORDER[:, None] - BIN_ORDER[None, :]) <= 32).astype(BF16)


def lag_table():
    lags = (np.arange(LAGS) - LAGS // 2)[:, None]
    angle = (BIN_ORDER[None, :] * lags % NT) * (2.0 * np.pi / NT)
    groups = (LAGS, NBINS // 16, 16)
    table = np.stack([np.cos(angle).reshape(groups), -np.sin(angle).reshape(groups)], axis=2)
    return (table.reshape(LAGS, 2 * NBINS) / np.sqrt(SEG * NBINS)).astype(np.float32).astype(BF16)


def split_rows(value, terms):
    parts = []
    for term in range(terms):
        part = value.astype(BF16)
        parts.append(part)
        if term < terms - 1:
            value = value - part.astype(F32)
    return parts


def whiten_kernel(
    base_ref, x_hbm, fir_hbm, even_hbm, odd_hbm, smooth_hbm, dead_ref, out_hbm,
    x_ref, fir_ref, even_ref, odd_ref, smooth_ref, seg_ref, turned_ref, sems,
):
    copies = [pltpu.make_async_copy(fir_hbm, fir_ref, sems.at[0])]
    for piece in range(4):
        lanes = pl.ds(PIECES[piece], PIECES[piece + 1] - PIECES[piece])
        copies.append(
            pltpu.make_async_copy(x_hbm.at[:, lanes], x_ref.at[:, lanes], sems.at[1 + piece])
        )
    copies.append(pltpu.make_async_copy(even_hbm, even_ref, sems.at[5]))
    copies.append(pltpu.make_async_copy(odd_hbm, odd_ref, sems.at[6]))
    copies.append(pltpu.make_async_copy(smooth_hbm, smooth_ref, sems.at[7]))
    for copy in copies:
        copy.start()
    copies[0].wait()
    edge = jnp.zeros((OWN, 128), F32)
    left_lanes = lax.broadcasted_iota(jnp.int32, (16 * OWN, 128), 1) < 64

    def filtered(parts, first, blocks, table):
        count = blocks * OWN
        windows = jnp.concatenate(
            [part[:, first + 512 * b : first + 512 * b + 256] for part in parts for b in range(blocks)],
            axis=0,
        )
        product = jnp.dot(windows, table, preferred_element_type=F32)
        return product[:count, :128] + (
            product[:count, 128:]
            + (
                product[count : 2 * count, :128]
                + (product[count : 2 * count, 128:] + product[2 * count :, :128])
            )
        )

    for piece in range(4):
        copies[1 + piece].wait()
        rows = x_ref[:, max(8192 * piece - 128, 0) : min(8192 * piece + 8320, 32768)]
        if piece == 0:
            rows = jnp.concatenate([edge, rows], axis=1)
        if piece == 3:
            rows = jnp.concatenate([rows, edge], axis=1)
        parts = split_rows(rows, 3)
        outer = filtered(parts, 0, 17, fir_ref[0:256])
        inner = filtered(parts, 256, 16, fir_ref[256:512])
        decimated = inner + jnp.where(left_lanes, outer[: 16 * OWN], outer[OWN:])
        for b in range(16):
            segment, part = 2 * piece + b // 8, b % 8
            seg_ref[segment * OWN : (segment + 1) * OWN, part * 128 : (part + 1) * 128] = (
                decimated[b * OWN : (b + 1) * OWN]
            )
    for copy in copies[5:]:
        copy.wait()
    rows = SEG * OWN

    def transform(folded, table_ref):
        terms = jnp.concatenate(split_rows(folded, 3), axis=0)
        high = jnp.dot(terms, table_ref[0], preferred_element_type=F32)
        mid = jnp.dot(terms[: 2 * rows], table_ref[1], preferred_element_type=F32)
        low = jnp.dot(terms[:rows], table_ref[2], preferred_element_type=F32)
        return high[:rows] + (
            high[rows : 2 * rows] + mid[:rows] + (high[2 * rows :] + mid[rows:] + low)
        )

    first, second = seg_ref[:, : NT // 2], seg_ref[:, NT // 2 :]
    even, odd = first + second, first - second
    first, second = even[:, : NT // 4], even[:, NT // 4 :]
    fours = transform(first + second, even_ref.at[0])
    twos = transform(first - second, even_ref.at[1])
    odds = transform(odd, odd_ref)
    real_part = jnp.concatenate([fours[:, :128], twos[:, :128], odds[:, :256]], axis=1)
    imag_part = jnp.concatenate([fours[:, 128:], twos[:, 128:], odds[:, 256:]], axis=1)
    power = real_part * real_part + imag_part * imag_part
    sums = jnp.dot(
        jnp.concatenate(split_rows(power, 2), axis=0), smooth_ref[...], preferred_element_type=F32
    )
    level = (sums[:rows] + sums[rows:]) / 65.0
    own_ids = base_ref[0] + (lax.broadcasted_iota(jnp.int32, (rows, 32), 0) & (OWN - 1))
    dead = jnp.max(jnp.where(dead_ref[...] == own_ids, 1.0, 0.0), axis=1, keepdims=True)
    scale = lax.rsqrt(level + 1e-06) * (1.0 - dead)
    real_part = real_part * scale
    imag_part = imag_part * scale
    chunk = lax.broadcasted_iota(jnp.int32, (OWN, 128), 1) >> 4
    sends = []
    for col in range(NBINS // 128):
        lanes = slice(col * 128, (col + 1) * 128)
        for kind, part in enumerate((real_part, imag_part)):
            tiles = [part[s * OWN : (s + 1) * OWN, lanes] for s in range(SEG)]
            for step in (1, 2, 4):
                low = (chunk & step) == 0
                for s in range(SEG):
                    if s & step == 0:
                        upper, lower = tiles[s], tiles[s + step]
                        tiles[s] = jnp.where(low, upper, pltpu.roll(lower, 16 * step, 1))
                        tiles[s + step] = jnp.where(low, pltpu.roll(upper, 128 - 16 * step, 1), lower)
            for member in range(SEG):
                first = (col * SEG + member) * 256 + kind * 128
                turned_ref[:, first : first + 128] = tiles[member].astype(BF16)
        wide = pl.ds(col * 2048, 2048)
        send = pltpu.make_async_copy(
            turned_ref.at[:, wide], out_hbm.at[:, wide], sems.at[8 + col]
        )
        send.start()
        sends.append(send)
    for send in sends:
        send.wait()


def pick_kernel(place_ref, sources_ref, *refs):
    parts, (out_ref, line_ref, wide_ref) = refs[:GROUP], refs[GROUP:]
    for step, part_ref in enumerate(parts):
        spot = pl.multiple_of(((place_ref[0] + step) & 3) * OWN, OWN)
        line_ref[pl.ds(spot, OWN), :] = part_ref[...]
    for tile in range(WIDE // 128):
        lanes = slice(tile * 128, (tile + 1) * 128)
        rows = jnp.concatenate([part_ref[:, lanes].astype(F32) for part_ref in parts], axis=0)
        first = tile // 4 * PITCH
        wide_ref[tile % 4, first : first + LINE] = rows
    for spot in range(PLANE):
        side, core, block = spot // 16, spot // 8 % 2, spot % 8
        index = 4 * ((block // 4) * 16 + (block % 4) * 4 + place_ref[0]) + core * 2 + side
        source = sources_ref[index]
        channel = (((source >> 4) - place_ref[0]) & 3) * OWN + (source & (OWN - 1))
        for col in range(4):
            rows = wide_ref[col, pl.ds(channel, 16, stride=PITCH), :]
            out_ref[spot, :, col * 128 : (col + 1) * 128] = rows.astype(BF16)


def keep_kernel(part_ref, out_ref):
    out_ref[...] = part_ref[...]


def hold_kernel(slot_ref, sources_ref, arrived_ref, out_ref):
    held = arrived_ref[sources_ref[slot_ref[0]] >> 6]
    for spot in range(SLOTS):
        out_ref[spot] = held


def corr_kernel(source_ref, own_ref, sibling_ref, lag_ref, out_ref, src_ref, cross_ref):
    src_ref[...] = source_ref[...].astype(F32)
    row = lax.broadcasted_iota(jnp.int32, (16, 256), 0)
    lane = lax.broadcasted_iota(jnp.int32, (16, 256), 1)
    real_mask = jnp.where(row == (lane & 15), 1.0, 0.0)
    imag_mask = jnp.where(lane < 128, real_mask, -real_mask)

    def group_step(line_row, side):
        group = line_row * 2 + side
        spread = []
        for slot in range(SLOTS):
            values = src_ref[slot, line_row : line_row + 1, side * 256 : (side + 1) * 256]
            swapped = jnp.concatenate([values[:, 128:], values[:, :128]], axis=1)
            spread.append((real_mask * values).astype(BF16))
            spread.append((imag_mask * swapped).astype(BF16))
        lanes = slice(group * 256, (group + 1) * 256)
        cross = lax.dot_general(
            jnp.concatenate(spread, axis=0),
            jnp.concatenate([own_ref[:, lanes], sibling_ref[:, lanes]], axis=0),
            (((1,), (1,)), ((), ())),
            preferred_element_type=F32,
        ).astype(BF16)
        rows = slice(group * 32, (group + 1) * 32)
        for slot in range(SLOTS):
            cross_ref[rows, slot * 128 : (slot + 1) * 128] = cross[slot * 32 : (slot + 1) * 32]

    for line_row in range(16):
        for side in range(2):
            group_step(line_row, side)
    for side in range(2):
        lanes = slice(side * 1024, (side + 1) * 1024)
        result = jnp.dot(
            lag_ref[...], cross_ref[:, lanes], preferred_element_type=F32
        ).astype(BF16)
        for block in range(8):
            for part in range(4):
                out_ref[part, block, :, side * 128 : (side + 1) * 128] = result[
                    part * 64 : (part + 1) * 64, block * 128 : (block + 1) * 128
                ]


def spread_kernel(in_ref, out_hbm, wide_ref, sems):
    sends = []
    for far_side in range(2):
        for core in range(2):
            for far in range(2):
                for pair in range(2):
                    left = in_ref[far_side, core, far, 2 * pair].astype(F32)
                    right = in_ref[far_side, core, far, 2 * pair + 1].astype(F32)
                    for part in range(4):
                        side, half = part // 2, part % 2
                        lanes = slice(part * LINE, (part + 1) * LINE)
                        spot = far_side * 1024 + (core ^ half) * 512 + far * 256 + pair * 128
                        wide_ref[2 * core + side, :, spot : spot + 128] = jnp.concatenate(
                            [left[:, lanes], right[:, lanes]], axis=1
                        )
            for side in range(2):
                spot = pl.ds(far_side * 1024, 1024)
                send = pltpu.make_async_copy(
                    wide_ref.at[2 * core + side, :, spot],
                    out_hbm.at[2 * core + side, :, spot],
                    sems.at[len(sends)],
                )
                send.start()
                sends.append(send)
    for send in sends:
        send.wait()


def vmem():
    return pl.BlockSpec(memory_space=pltpu.VMEM)


def smem():
    return pl.BlockSpec(memory_space=pltpu.SMEM)


def whole():
    return pl.BlockSpec(memory_space=pl.ANY)


SMALL = pltpu.CompilerParams(vmem_limit_bytes=12 * 1024 * 1024)
MEDIUM = pltpu.CompilerParams(vmem_limit_bytes=20 * 1024 * 1024)
FULL = pltpu.CompilerParams(vmem_limit_bytes=60 * 1024 * 1024)


def call_whiten(base, records, dead_list):
    return pl.pallas_call(
        whiten_kernel,
        out_shape=jax.ShapeDtypeStruct((OWN, WIDE), BF16),
        in_specs=[smem(), whole(), whole(), whole(), whole(), whole(), vmem()],
        out_specs=whole(),
        scratch_shapes=[
            pltpu.VMEM((OWN, 32768), F32),
            pltpu.VMEM((512, 256), BF16),
            pltpu.VMEM((2, 3, NT // 4, NBINS // 2), BF16),
            pltpu.VMEM((3, NT // 2, NBINS), BF16),
            pltpu.VMEM((NBINS, NBINS), BF16),
            pltpu.VMEM((SEG * OWN, NT), F32),
            pltpu.VMEM((OWN, WIDE), BF16),
            pltpu.SemaphoreType.DMA((12,)),
        ],
        compiler_params=FULL,
        name="whiten",
    )(
        base,
        records,
        jnp.asarray(fir_table()),
        jnp.asarray(even_table()),
        jnp.asarray(odd_table()),
        jnp.asarray(smooth_table()),
        dead_list.reshape(1, 32),
    )


def call_pick(place, sources, parts):
    return pl.pallas_call(
        pick_kernel,
        out_shape=(
            jax.ShapeDtypeStruct((PLANE, 2 * SEG, NBINS), BF16),
            jax.ShapeDtypeStruct((LINE, WIDE), BF16),
        ),
        in_specs=[smem(), smem()] + [vmem()] * GROUP,
        out_specs=(vmem(), vmem()),
        scratch_shapes=[pltpu.VMEM((4, 17 * LINE, 128), F32)],
        compiler_params=SMALL,
        name="pick",
    )(place, sources, *parts)


def call_keep(part):
    return pl.pallas_call(
        keep_kernel,
        out_shape=jax.ShapeDtypeStruct((OWN, WIDE), BF16),
        in_specs=[vmem()],
        out_specs=vmem(),
        compiler_params=SMALL,
        cost_estimate=pl.CostEstimate(flops=0, bytes_accessed=1048576, transcendentals=0),
        name="keep",
    )(part)


def call_hold(slot, sources, arrived):
    return pl.pallas_call(
        hold_kernel,
        out_shape=jax.ShapeDtypeStruct((SLOTS, 2 * SEG, NBINS), BF16),
        in_specs=[smem(), smem(), vmem()],
        out_specs=vmem(),
        compiler_params=SMALL,
        name="hold",
    )(slot, sources, arrived)


def call_corr(source_spectra, own, sibling):
    return pl.pallas_call(
        corr_kernel,
        out_shape=jax.ShapeDtypeStruct((4, 8, LAGS // 4, 4 * LINE), BF16),
        in_specs=[vmem(), vmem(), vmem(), vmem()],
        out_specs=vmem(),
        scratch_shapes=[
            pltpu.VMEM((SLOTS, 16, 512), F32),
            pltpu.VMEM((2 * NBINS, SLOTS * 2 * LINE), BF16),
        ],
        compiler_params=MEDIUM,
        name="correlate",
    )(source_spectra, own, sibling, jnp.asarray(lag_table()))


def call_spread(gathered):
    return pl.pallas_call(
        spread_kernel,
        out_shape=jax.ShapeDtypeStruct((4, LAGS // 4, PLANE * LINE), F32),
        in_specs=[vmem()],
        out_specs=whole(),
        scratch_shapes=[
            pltpu.VMEM((4, LAGS // 4, PLANE * LINE), F32),
            pltpu.SemaphoreType.DMA((8,)),
        ],
        compiler_params=SMALL,
        name="spread",
    )(gathered)


def shards(records, sources, dead_list):
    xl_pos = lax.axis_index("xl")
    core_pos = lax.axis_index("core")
    xh_pos = lax.axis_index("xh")
    z_pos = lax.axis_index("z")
    y_pos = lax.axis_index("y")
    chan_pos = (xh_pos * 4 + z_pos) * 4 + y_pos
    device = (xl_pos * 2 + core_pos) * 32 + chan_pos
    own_slot = 4 * chan_pos + core_pos * 2 + xl_pos
    whitened = call_whiten((device * OWN).reshape(1), records, dead_list)
    parts = {0: call_keep(whitened)}
    for step in (2, 1, 3):
        parts[step] = lax.ppermute(whitened, "y", [(i, (i - step) % GROUP) for i in range(GROUP)])
    parts = [parts[step] for step in range(GROUP)]
    picked, line = call_pick(y_pos.reshape(1), sources, parts)
    arrived = lax.all_to_all(picked, PLANE_AXES, 0, 0, tiled=True)
    arrived, sent_line = lax.optimization_barrier((arrived, line))
    sibling_line = lax.ppermute(sent_line, "core", [(0, 1), (1, 0)])
    held = call_hold(own_slot.reshape(1), sources, arrived)
    source_spectra = lax.all_to_all(held, SIDE_AXES, 0, 0, tiled=True)
    blocks = call_corr(source_spectra, sent_line, sibling_line)
    gathered = lax.all_to_all(
        blocks.reshape(PLANE, LAGS // 4, 4 * LINE), PLANE_AXES, 0, 0, tiled=True
    )
    return call_spread(gathered.reshape(2, 2, 2, 4, LAGS // 4, 4 * LINE))


def solution(mesh):
    inner = Mesh(mesh.devices.reshape(2, 2, 2, 4, 4), AXES)
    return jax.shard_map(
        shards,
        mesh=inner,
        in_specs=(P(AXES, None), P(), P()),
        out_specs=P(("xh", "z", "y"), ("xl", "core"), None),
        check_vma=False,
    )
```

```python
import numpy as np
import jax
import jax.numpy as jnp
from jax import lax
from jax.experimental import pallas as pl
from jax.experimental.pallas import tpu as pltpu
from jax.sharding import Mesh, PartitionSpec as P

NT = 1024
LAGS = 256
SEG = 8
NBINS = 512
OWN = 16
GROUP = 4
PLANE = 32
LINE = GROUP * OWN
AXES = ("xl", "core", "xh", "z", "y")
PLANE_AXES = ("xl", "core", "xh", "z")
SIDE_AXES = ("xl", "xh", "z")
SLOTS = 16
WIDE = 2 * SEG * NBINS
PITCH = LINE + 1
BIN_ORDER = np.concatenate([np.arange(4, 513, 4), np.arange(2, 512, 4), np.arange(1, 512, 2)])
PIECES = (0, 8320, 16512, 24704, 32768)
F32 = jnp.float32
BF16 = jnp.bfloat16


def split_table(table, terms):
    left = table.astype(np.float64)
    parts = []
    for _ in range(terms):
        part = left.astype(np.float32).astype(BF16)
        parts.append(part)
        left = left - part.astype(np.float64)
    return parts


def fir_table():
    row = np.arange(768)[:, None]
    col = np.arange(128)[None, :]
    offset = 4 * col + 255 - row
    inside = (offset >= 0) & (offset <= 254)
    tap = offset.astype(np.float64)
    hamming = 0.54 - 0.46 * np.cos(2.0 * np.pi * tap / 254.0)
    values = np.where(inside, 0.2 * np.sinc(0.2 * (tap - 127.0)) * hamming, 0.0)
    outer = np.concatenate([values[:256, :64], values[512:, 64:]], axis=1)
    return np.concatenate(
        [np.concatenate(split_table(part, 2), axis=1) for part in (outer, values[256:512])], axis=0
    )


def dft_table(samples, bins):
    angle = (np.arange(samples)[:, None] * bins[None, :] % NT) * (2.0 * np.pi / NT)
    return np.stack(split_table(np.concatenate([np.cos(angle), -np.sin(angle)], axis=1), 3))


def even_table():
    return np.stack([dft_table(256, BIN_ORDER[:128]), dft_table(256, BIN_ORDER[128:256])])


def odd_table():
    return dft_table(512, BIN_ORDER[256:])


def smooth_table():
    return (np.abs(BIN_ORDER[:, None] - BIN_ORDER[None, :]) <= 32).astype(BF16)


def lag_table():
    lags = (np.arange(LAGS) - LAGS // 2)[:, None]
    angle = (BIN_ORDER[None, :] * lags % NT) * (2.0 * np.pi / NT)
    groups = (LAGS, NBINS // 16, 16)
    table = np.stack([np.cos(angle).reshape(groups), -np.sin(angle).reshape(groups)], axis=2)
    return (table.reshape(LAGS, 2 * NBINS) / np.sqrt(SEG * NBINS)).astype(np.float32).astype(BF16)


def split_rows(value, terms):
    parts = []
    for term in range(terms):
        part = value.astype(BF16)
        parts.append(part)
        if term < terms - 1:
            value = value - part.astype(F32)
    return parts


def whiten_kernel(
    base_ref, x_hbm, fir_hbm, even_hbm, odd_hbm, smooth_hbm, dead_ref, out_hbm,
    x_ref, fir_ref, even_ref, odd_ref, smooth_ref, seg_ref, turned_ref, sems,
):
    copies = [pltpu.make_async_copy(fir_hbm, fir_ref, sems.at[0])]
    for piece in range(4):
        lanes = pl.ds(PIECES[piece], PIECES[piece + 1] - PIECES[piece])
        copies.append(
            pltpu.make_async_copy(x_hbm.at[:, lanes], x_ref.at[:, lanes], sems.at[1 + piece])
        )
    copies.append(pltpu.make_async_copy(even_hbm, even_ref, sems.at[5]))
    copies.append(pltpu.make_async_copy(odd_hbm, odd_ref, sems.at[6]))
    copies.append(pltpu.make_async_copy(smooth_hbm, smooth_ref, sems.at[7]))
    for copy in copies:
        copy.start()
    copies[0].wait()
    edge = jnp.zeros((OWN, 128), F32)
    left_lanes = lax.broadcasted_iota(jnp.int32, (16 * OWN, 128), 1) < 64

    def filtered(parts, first, blocks, table):
        count = blocks * OWN
        windows = jnp.concatenate(
            [part[:, first + 512 * b : first + 512 * b + 256] for part in parts for b in range(blocks)],
            axis=0,
        )
        product = jnp.dot(windows, table, preferred_element_type=F32)
        return product[:count, :128] + (
            product[:count, 128:]
            + (
                product[count : 2 * count, :128]
                + (product[count : 2 * count, 128:] + product[2 * count :, :128])
            )
        )

    for piece in range(4):
        copies[1 + piece].wait()
        rows = x_ref[:, max(8192 * piece - 128, 0) : min(8192 * piece + 8320, 32768)]
        if piece == 0:
            rows = jnp.concatenate([edge, rows], axis=1)
        if piece == 3:
            rows = jnp.concatenate([rows, edge], axis=1)
        parts = split_rows(rows, 3)
        outer = filtered(parts, 0, 17, fir_ref[0:256])
        inner = filtered(parts, 256, 16, fir_ref[256:512])
        decimated = inner + jnp.where(left_lanes, outer[: 16 * OWN], outer[OWN:])
        for b in range(16):
            segment, part = 2 * piece + b // 8, b % 8
            seg_ref[segment * OWN : (segment + 1) * OWN, part * 128 : (part + 1) * 128] = (
                decimated[b * OWN : (b + 1) * OWN]
            )
    for copy in copies[5:]:
        copy.wait()
    rows = SEG * OWN

    def transform(folded, table_ref):
        terms = jnp.concatenate(split_rows(folded, 3), axis=0)
        high = jnp.dot(terms, table_ref[0], preferred_element_type=F32)
        mid = jnp.dot(terms[: 2 * rows], table_ref[1], preferred_element_type=F32)
        low = jnp.dot(terms[:rows], table_ref[2], preferred_element_type=F32)
        return high[:rows] + (
            high[rows : 2 * rows] + mid[:rows] + (high[2 * rows :] + mid[rows:] + low)
        )

    first, second = seg_ref[:, : NT // 2], seg_ref[:, NT // 2 :]
    even, odd = first + second, first - second
    first, second = even[:, : NT // 4], even[:, NT // 4 :]
    fours = transform(first + second, even_ref.at[0])
    twos = transform(first - second, even_ref.at[1])
    odds = transform(odd, odd_ref)
    real_part = jnp.concatenate([fours[:, :128], twos[:, :128], odds[:, :256]], axis=1)
    imag_part = jnp.concatenate([fours[:, 128:], twos[:, 128:], odds[:, 256:]], axis=1)
    power = real_part * real_part + imag_part * imag_part
    sums = jnp.dot(
        jnp.concatenate(split_rows(power, 2), axis=0), smooth_ref[...], preferred_element_type=F32
    )
    level = (sums[:rows] + sums[rows:]) / 65.0
    own_ids = base_ref[0] + (lax.broadcasted_iota(jnp.int32, (rows, 32), 0) & (OWN - 1))
    dead = jnp.max(jnp.where(dead_ref[...] == own_ids, 1.0, 0.0), axis=1, keepdims=True)
    scale = lax.rsqrt(level + 1e-06) * (1.0 - dead)
    real_part = real_part * scale
    imag_part = imag_part * scale
    chunk = lax.broadcasted_iota(jnp.int32, (OWN, 128), 1) >> 4
    sends = []
    for col in range(NBINS // 128):
        lanes = slice(col * 128, (col + 1) * 128)
        for kind, part in enumerate((real_part, imag_part)):
            tiles = [part[s * OWN : (s + 1) * OWN, lanes] for s in range(SEG)]
            for step in (1, 2, 4):
                low = (chunk & step) == 0
                for s in range(SEG):
                    if s & step == 0:
                        upper, lower = tiles[s], tiles[s + step]
                        tiles[s] = jnp.where(low, upper, pltpu.roll(lower, 16 * step, 1))
                        tiles[s + step] = jnp.where(low, pltpu.roll(upper, 128 - 16 * step, 1), lower)
            for member in range(SEG):
                first = (col * SEG + member) * 256 + kind * 128
                turned_ref[:, first : first + 128] = tiles[member].astype(BF16)
        wide = pl.ds(col * 2048, 2048)
        send = pltpu.make_async_copy(
            turned_ref.at[:, wide], out_hbm.at[:, wide], sems.at[8 + col]
        )
        send.start()
        sends.append(send)
    for send in sends:
        send.wait()


def pick_kernel(place_ref, sources_ref, *refs):
    own_ref, after_ref, left_ref, right_ref, before_ref, out_ref, line_ref, wide_ref = refs
    cut = WIDE // 2
    for half, across_ref in enumerate((left_ref, right_ref)):
        lanes = slice(half * cut, (half + 1) * cut)
        halves = (own_ref[:, lanes], after_ref[:, lanes], across_ref[...], before_ref[:, lanes])
        for step, value in enumerate(halves):
            spot = pl.multiple_of(((place_ref[0] + step) & 3) * OWN, OWN)
            line_ref[pl.ds(spot, OWN), lanes] = value
    for tile in range(WIDE // 128):
        lanes = slice(tile * 128, (tile + 1) * 128)
        near = slice(tile * 128 % cut, tile * 128 % cut + 128)
        across = (left_ref if tile * 128 < cut else right_ref)[:, near]
        values = (own_ref[:, lanes], after_ref[:, lanes], across, before_ref[:, lanes])
        rows = jnp.concatenate([value.astype(F32) for value in values], axis=0)
        first = tile // 4 * PITCH
        wide_ref[tile % 4, first : first + LINE] = rows
    for spot in range(PLANE):
        side, core, block = spot // 16, spot // 8 % 2, spot % 8
        index = 4 * ((block // 4) * 16 + (block % 4) * 4 + place_ref[0]) + core * 2 + side
        source = sources_ref[index]
        channel = (((source >> 4) - place_ref[0]) & 3) * OWN + (source & (OWN - 1))
        for col in range(4):
            rows = wide_ref[col, pl.ds(channel, 16, stride=PITCH), :]
            out_ref[spot, :, col * 128 : (col + 1) * 128] = rows.astype(BF16)


def keep_kernel(part_ref, out_ref):
    out_ref[...] = part_ref[...]


def hold_kernel(slot_ref, sources_ref, arrived_ref, out_ref):
    held = arrived_ref[sources_ref[slot_ref[0]] >> 6]
    for spot in range(SLOTS):
        out_ref[spot] = held


def corr_kernel(source_ref, own_ref, sibling_ref, lag_ref, out_ref, src_ref, cross_ref):
    src_ref[...] = source_ref[...].astype(F32)
    row = lax.broadcasted_iota(jnp.int32, (16, 256), 0)
    lane = lax.broadcasted_iota(jnp.int32, (16, 256), 1)
    real_mask = jnp.where(row == (lane & 15), 1.0, 0.0)
    imag_mask = jnp.where(lane < 128, real_mask, -real_mask)

    def group_step(line_row, side):
        group = line_row * 2 + side
        spread = []
        for slot in range(SLOTS):
            values = src_ref[slot, line_row : line_row + 1, side * 256 : (side + 1) * 256]
            swapped = jnp.concatenate([values[:, 128:], values[:, :128]], axis=1)
            spread.append((real_mask * values).astype(BF16))
            spread.append((imag_mask * swapped).astype(BF16))
        lanes = slice(group * 256, (group + 1) * 256)
        cross = lax.dot_general(
            jnp.concatenate(spread, axis=0),
            jnp.concatenate([own_ref[:, lanes], sibling_ref[:, lanes]], axis=0),
            (((1,), (1,)), ((), ())),
            preferred_element_type=F32,
        ).astype(BF16)
        rows = slice(group * 32, (group + 1) * 32)
        for slot in range(SLOTS):
            cross_ref[rows, slot * 128 : (slot + 1) * 128] = cross[slot * 32 : (slot + 1) * 32]

    for line_row in range(16):
        for side in range(2):
            group_step(line_row, side)
    for side in range(2):
        lanes = slice(side * 1024, (side + 1) * 1024)
        result = jnp.dot(
            lag_ref[...], cross_ref[:, lanes], preferred_element_type=F32
        ).astype(BF16)
        for block in range(8):
            for part in range(4):
                out_ref[part, block, :, side * 128 : (side + 1) * 128] = result[
                    part * 64 : (part + 1) * 64, block * 128 : (block + 1) * 128
                ]


def spread_kernel(in_ref, out_hbm, wide_ref, sems):
    sends = []
    for far_side in range(2):
        for core in range(2):
            for far in range(2):
                for pair in range(2):
                    left = in_ref[far_side, core, far, 2 * pair].astype(F32)
                    right = in_ref[far_side, core, far, 2 * pair + 1].astype(F32)
                    for part in range(4):
                        side, half = part // 2, part % 2
                        lanes = slice(part * LINE, (part + 1) * LINE)
                        spot = far_side * 1024 + (core ^ half) * 512 + far * 256 + pair * 128
                        wide_ref[2 * core + side, :, spot : spot + 128] = jnp.concatenate(
                            [left[:, lanes], right[:, lanes]], axis=1
                        )
            for side in range(2):
                spot = pl.ds(far_side * 1024, 1024)
                send = pltpu.make_async_copy(
                    wide_ref.at[2 * core + side, :, spot],
                    out_hbm.at[2 * core + side, :, spot],
                    sems.at[len(sends)],
                )
                send.start()
                sends.append(send)
    for send in sends:
        send.wait()


def vmem():
    return pl.BlockSpec(memory_space=pltpu.VMEM)


def smem():
    return pl.BlockSpec(memory_space=pltpu.SMEM)


def whole():
    return pl.BlockSpec(memory_space=pl.ANY)


SMALL = pltpu.CompilerParams(vmem_limit_bytes=12 * 1024 * 1024)
MEDIUM = pltpu.CompilerParams(vmem_limit_bytes=20 * 1024 * 1024)
FULL = pltpu.CompilerParams(vmem_limit_bytes=60 * 1024 * 1024)


def call_whiten(base, records, dead_list):
    return pl.pallas_call(
        whiten_kernel,
        out_shape=jax.ShapeDtypeStruct((OWN, WIDE), BF16),
        in_specs=[smem(), whole(), whole(), whole(), whole(), whole(), vmem()],
        out_specs=whole(),
        scratch_shapes=[
            pltpu.VMEM((OWN, 32768), F32),
            pltpu.VMEM((512, 256), BF16),
            pltpu.VMEM((2, 3, NT // 4, NBINS // 2), BF16),
            pltpu.VMEM((3, NT // 2, NBINS), BF16),
            pltpu.VMEM((NBINS, NBINS), BF16),
            pltpu.VMEM((SEG * OWN, NT), F32),
            pltpu.VMEM((OWN, WIDE), BF16),
            pltpu.SemaphoreType.DMA((12,)),
        ],
        compiler_params=FULL,
        name="whiten",
    )(
        base,
        records,
        jnp.asarray(fir_table()),
        jnp.asarray(even_table()),
        jnp.asarray(odd_table()),
        jnp.asarray(smooth_table()),
        dead_list.reshape(1, 32),
    )


def call_pick(place, sources, parts):
    return pl.pallas_call(
        pick_kernel,
        out_shape=(
            jax.ShapeDtypeStruct((PLANE, 2 * SEG, NBINS), BF16),
            jax.ShapeDtypeStruct((LINE, WIDE), BF16),
        ),
        in_specs=[smem(), smem()] + [vmem()] * 5,
        out_specs=(vmem(), vmem()),
        scratch_shapes=[pltpu.VMEM((4, 17 * LINE, 128), F32)],
        compiler_params=SMALL,
        name="pick",
    )(place, sources, *parts)


def call_keep(part):
    return pl.pallas_call(
        keep_kernel,
        out_shape=jax.ShapeDtypeStruct((OWN, WIDE), BF16),
        in_specs=[vmem()],
        out_specs=vmem(),
        compiler_params=SMALL,
        cost_estimate=pl.CostEstimate(flops=0, bytes_accessed=1048576, transcendentals=0),
        name="keep",
    )(part)


def call_hold(slot, sources, arrived):
    return pl.pallas_call(
        hold_kernel,
        out_shape=jax.ShapeDtypeStruct((SLOTS, 2 * SEG, NBINS), BF16),
        in_specs=[smem(), smem(), vmem()],
        out_specs=vmem(),
        compiler_params=SMALL,
        name="hold",
    )(slot, sources, arrived)


def call_corr(source_spectra, own, sibling):
    return pl.pallas_call(
        corr_kernel,
        out_shape=jax.ShapeDtypeStruct((4, 8, LAGS // 4, 4 * LINE), BF16),
        in_specs=[vmem(), vmem(), vmem(), vmem()],
        out_specs=vmem(),
        scratch_shapes=[
            pltpu.VMEM((SLOTS, 16, 512), F32),
            pltpu.VMEM((2 * NBINS, SLOTS * 2 * LINE), BF16),
        ],
        compiler_params=MEDIUM,
        name="correlate",
    )(source_spectra, own, sibling, jnp.asarray(lag_table()))


def call_spread(gathered):
    return pl.pallas_call(
        spread_kernel,
        out_shape=jax.ShapeDtypeStruct((4, LAGS // 4, PLANE * LINE), F32),
        in_specs=[vmem()],
        out_specs=whole(),
        scratch_shapes=[
            pltpu.VMEM((4, LAGS // 4, PLANE * LINE), F32),
            pltpu.SemaphoreType.DMA((8,)),
        ],
        compiler_params=SMALL,
        name="spread",
    )(gathered)


def shards(records, sources, dead_list):
    xl_pos = lax.axis_index("xl")
    core_pos = lax.axis_index("core")
    xh_pos = lax.axis_index("xh")
    z_pos = lax.axis_index("z")
    y_pos = lax.axis_index("y")
    chan_pos = (xh_pos * 4 + z_pos) * 4 + y_pos
    device = (xl_pos * 2 + core_pos) * 32 + chan_pos
    own_slot = 4 * chan_pos + core_pos * 2 + xl_pos
    whitened = call_whiten((device * OWN).reshape(1), records, dead_list)
    up = [(i, (i + 1) % GROUP) for i in range(GROUP)]
    down = [(i, (i - 1) % GROUP) for i in range(GROUP)]
    after = lax.ppermute(whitened, "y", down)
    before = lax.ppermute(whitened, "y", up)
    left = lax.ppermute(after[:, : WIDE // 2], "y", down)
    right = lax.ppermute(before[:, WIDE // 2 :], "y", up)
    parts = [call_keep(whitened), after, left, right, before]
    picked, line = call_pick(y_pos.reshape(1), sources, parts)
    arrived = lax.all_to_all(picked, PLANE_AXES, 0, 0, tiled=True)
    arrived, sent_line = lax.optimization_barrier((arrived, line))
    sibling_line = lax.ppermute(sent_line, "core", [(0, 1), (1, 0)])
    held = call_hold(own_slot.reshape(1), sources, arrived)
    source_spectra = lax.all_to_all(held, SIDE_AXES, 0, 0, tiled=True)
    blocks = call_corr(source_spectra, sent_line, sibling_line)
    gathered = lax.all_to_all(
        blocks.reshape(PLANE, LAGS // 4, 4 * LINE), PLANE_AXES, 0, 0, tiled=True
    )
    return call_spread(gathered.reshape(2, 2, 2, 4, LAGS // 4, 4 * LINE))


def solution(mesh):
    inner = Mesh(mesh.devices.reshape(2, 2, 2, 4, 4), AXES)
    return jax.shard_map(
        shards,
        mesh=inner,
        in_specs=(P(AXES, None), P(), P()),
        out_specs=P(("xh", "z", "y"), ("xl", "core"), None),
        check_vma=False,
    )
```

```python
import numpy as np
import jax
import jax.numpy as jnp
from jax import lax
from jax.experimental import pallas as pl
from jax.experimental.pallas import tpu as pltpu
from jax.sharding import Mesh, PartitionSpec as P

NT = 1024
LAGS = 256
SEG = 8
NBINS = 512
OWN = 16
GROUP = 4
PLANE = 32
LINE = GROUP * OWN
AXES = ("xl", "core", "xh", "z", "y")
PLANE_AXES = ("xl", "core", "xh", "z")
SIDE_AXES = ("xl", "xh", "z")
SLOTS = 16
WIDE = 2 * SEG * NBINS
PITCH = LINE + 1
BIN_ORDER = np.concatenate([np.arange(4, 513, 4), np.arange(2, 512, 4), np.arange(1, 512, 2)])
PIECES = (0, 8320, 16512, 24704, 32768)
F32 = jnp.float32
BF16 = jnp.bfloat16


def split_table(table, terms):
    left = table.astype(np.float64)
    parts = []
    for _ in range(terms):
        part = left.astype(np.float32).astype(BF16)
        parts.append(part)
        left = left - part.astype(np.float64)
    return parts


def fir_table():
    row = np.arange(768)[:, None]
    col = np.arange(128)[None, :]
    offset = 4 * col + 255 - row
    inside = (offset >= 0) & (offset <= 254)
    tap = offset.astype(np.float64)
    hamming = 0.54 - 0.46 * np.cos(2.0 * np.pi * tap / 254.0)
    values = np.where(inside, 0.2 * np.sinc(0.2 * (tap - 127.0)) * hamming, 0.0)
    outer = np.concatenate([values[:256, :64], values[512:, 64:]], axis=1)
    return np.concatenate(
        [np.concatenate(split_table(part, 2), axis=1) for part in (outer, values[256:512])], axis=0
    )


def dft_table(samples, bins):
    angle = (np.arange(samples)[:, None] * bins[None, :] % NT) * (2.0 * np.pi / NT)
    return np.stack(split_table(np.concatenate([np.cos(angle), -np.sin(angle)], axis=1), 3))


def even_table():
    return np.stack([dft_table(256, BIN_ORDER[:128]), dft_table(256, BIN_ORDER[128:256])])


def odd_table():
    return dft_table(512, BIN_ORDER[256:])


def smooth_table():
    return (np.abs(BIN_ORDER[:, None] - BIN_ORDER[None, :]) <= 32).astype(BF16)


def lag_table():
    lags = (np.arange(LAGS) - LAGS // 2)[:, None]
    angle = (BIN_ORDER[None, :] * lags % NT) * (2.0 * np.pi / NT)
    groups = (LAGS, NBINS // 16, 16)
    table = np.stack([np.cos(angle).reshape(groups), -np.sin(angle).reshape(groups)], axis=2)
    return (table.reshape(LAGS, 2 * NBINS) / np.sqrt(SEG * NBINS)).astype(np.float32).astype(BF16)


def split_rows(value, terms):
    parts = []
    for term in range(terms):
        part = value.astype(BF16)
        parts.append(part)
        if term < terms - 1:
            value = value - part.astype(F32)
    return parts


def whiten_kernel(
    base_ref, x_hbm, fir_hbm, even_hbm, odd_hbm, smooth_hbm, dead_ref, out_hbm,
    x_ref, fir_ref, even_ref, odd_ref, smooth_ref, seg_ref, turned_ref, sems,
):
    copies = [pltpu.make_async_copy(fir_hbm, fir_ref, sems.at[0])]
    for piece in range(4):
        lanes = pl.ds(PIECES[piece], PIECES[piece + 1] - PIECES[piece])
        copies.append(
            pltpu.make_async_copy(x_hbm.at[:, lanes], x_ref.at[:, lanes], sems.at[1 + piece])
        )
    copies.append(pltpu.make_async_copy(even_hbm, even_ref, sems.at[5]))
    copies.append(pltpu.make_async_copy(odd_hbm, odd_ref, sems.at[6]))
    copies.append(pltpu.make_async_copy(smooth_hbm, smooth_ref, sems.at[7]))
    for copy in copies:
        copy.start()
    copies[0].wait()
    edge = jnp.zeros((OWN, 128), F32)
    left_lanes = lax.broadcasted_iota(jnp.int32, (16 * OWN, 128), 1) < 64

    def filtered(parts, first, blocks, table):
        count = blocks * OWN
        windows = jnp.concatenate(
            [part[:, first + 512 * b : first + 512 * b + 256] for part in parts for b in range(blocks)],
            axis=0,
        )
        product = jnp.dot(windows, table, preferred_element_type=F32)
        return product[:count, :128] + (
            product[:count, 128:]
            + (
                product[count : 2 * count, :128]
                + (product[count : 2 * count, 128:] + product[2 * count :, :128])
            )
        )

    for piece in range(4):
        copies[1 + piece].wait()
        rows = x_ref[:, max(8192 * piece - 128, 0) : min(8192 * piece + 8320, 32768)]
        if piece == 0:
            rows = jnp.concatenate([edge, rows], axis=1)
        if piece == 3:
            rows = jnp.concatenate([rows, edge], axis=1)
        parts = split_rows(rows, 3)
        outer = filtered(parts, 0, 17, fir_ref[0:256])
        inner = filtered(parts, 256, 16, fir_ref[256:512])
        decimated = inner + jnp.where(left_lanes, outer[: 16 * OWN], outer[OWN:])
        for b in range(16):
            segment, part = 2 * piece + b // 8, b % 8
            seg_ref[segment * OWN : (segment + 1) * OWN, part * 128 : (part + 1) * 128] = (
                decimated[b * OWN : (b + 1) * OWN]
            )
    for copy in copies[5:]:
        copy.wait()
    rows = SEG * OWN

    def transform(folded, table_ref):
        terms = jnp.concatenate(split_rows(folded, 3), axis=0)
        high = jnp.dot(terms, table_ref[0], preferred_element_type=F32)
        mid = jnp.dot(terms[: 2 * rows], table_ref[1], preferred_element_type=F32)
        low = jnp.dot(terms[:rows], table_ref[2], preferred_element_type=F32)
        return high[:rows] + (
            high[rows : 2 * rows] + mid[:rows] + (high[2 * rows :] + mid[rows:] + low)
        )

    first, second = seg_ref[:, : NT // 2], seg_ref[:, NT // 2 :]
    even, odd = first + second, first - second
    first, second = even[:, : NT // 4], even[:, NT // 4 :]
    fours = transform(first + second, even_ref.at[0])
    twos = transform(first - second, even_ref.at[1])
    odds = transform(odd, odd_ref)
    real_part = jnp.concatenate([fours[:, :128], twos[:, :128], odds[:, :256]], axis=1)
    imag_part = jnp.concatenate([fours[:, 128:], twos[:, 128:], odds[:, 256:]], axis=1)
    power = real_part * real_part + imag_part * imag_part
    sums = jnp.dot(
        jnp.concatenate(split_rows(power, 2), axis=0), smooth_ref[...], preferred_element_type=F32
    )
    level = (sums[:rows] + sums[rows:]) / 65.0
    own_ids = base_ref[0] + (lax.broadcasted_iota(jnp.int32, (rows, 32), 0) & (OWN - 1))
    dead = jnp.max(jnp.where(dead_ref[...] == own_ids, 1.0, 0.0), axis=1, keepdims=True)
    scale = lax.rsqrt(level + 1e-06) * (1.0 - dead)
    real_part = real_part * scale
    imag_part = imag_part * scale
    chunk = lax.broadcasted_iota(jnp.int32, (OWN, 128), 1) >> 4
    sends = []
    for col in range(NBINS // 128):
        lanes = slice(col * 128, (col + 1) * 128)
        for kind, part in enumerate((real_part, imag_part)):
            tiles = [part[s * OWN : (s + 1) * OWN, lanes] for s in range(SEG)]
            for step in (1, 2, 4):
                low = (chunk & step) == 0
                for s in range(SEG):
                    if s & step == 0:
                        upper, lower = tiles[s], tiles[s + step]
                        tiles[s] = jnp.where(low, upper, pltpu.roll(lower, 16 * step, 1))
                        tiles[s + step] = jnp.where(low, pltpu.roll(upper, 128 - 16 * step, 1), lower)
            for member in range(SEG):
                first = (col * SEG + member) * 256 + kind * 128
                turned_ref[:, first : first + 128] = tiles[member].astype(BF16)
        wide = pl.ds(col * 2048, 2048)
        send = pltpu.make_async_copy(
            turned_ref.at[:, wide], out_hbm.at[:, wide], sems.at[8 + col]
        )
        send.start()
        sends.append(send)
    for send in sends:
        send.wait()


def pick_kernel(place_ref, sources_ref, *refs):
    own_ref, after_ref, left_ref, right_ref, before_ref, out_ref, line_ref, wide_ref = refs
    cut = WIDE // 2
    for half, across_ref in enumerate((left_ref, right_ref)):
        lanes = slice(half * cut, (half + 1) * cut)
        halves = (own_ref[:, lanes], after_ref[:, lanes], across_ref[...], before_ref[:, lanes])
        for step, value in enumerate(halves):
            spot = pl.multiple_of(((place_ref[0] + step) & 3) * OWN, OWN)
            line_ref[pl.ds(spot, OWN), lanes] = value
    for tile in range(WIDE // 128):
        lanes = slice(tile * 128, (tile + 1) * 128)
        near = slice(tile * 128 % cut, tile * 128 % cut + 128)
        across = (left_ref if tile * 128 < cut else right_ref)[:, near]
        values = (own_ref[:, lanes], after_ref[:, lanes], across, before_ref[:, lanes])
        rows = jnp.concatenate([value.astype(F32) for value in values], axis=0)
        first = tile // 4 * PITCH
        wide_ref[tile % 4, first : first + LINE] = rows
    for spot in range(PLANE):
        side, core, block = spot // 16, spot // 8 % 2, spot % 8
        index = 4 * ((block // 4) * 16 + (block % 4) * 4 + place_ref[0]) + core * 2 + side
        source = sources_ref[index]
        channel = (((source >> 4) - place_ref[0]) & 3) * OWN + (source & (OWN - 1))
        for col in range(4):
            rows = wide_ref[col, pl.ds(channel, 16, stride=PITCH), :]
            out_ref[spot, :, col * 128 : (col + 1) * 128] = rows.astype(BF16)


def keep_kernel(part_ref, out_ref):
    out_ref[...] = part_ref[...]


def hold_kernel(slot_ref, sources_ref, arrived_ref, out_ref):
    held = arrived_ref[sources_ref[slot_ref[0]] >> 6]
    for spot in range(SLOTS):
        out_ref[spot] = held


def corr_kernel(source_ref, own_ref, sibling_ref, lag_ref, out_ref, src_ref, cross_ref):
    src_ref[...] = source_ref[...].astype(F32)
    row = lax.broadcasted_iota(jnp.int32, (16, 256), 0)
    lane = lax.broadcasted_iota(jnp.int32, (16, 256), 1)
    real_mask = jnp.where(row == (lane & 15), 1.0, 0.0)
    imag_mask = jnp.where(lane < 128, real_mask, -real_mask)

    def group_step(line_row, side):
        group = line_row * 2 + side
        spread = []
        for slot in range(SLOTS):
            values = src_ref[slot, line_row : line_row + 1, side * 256 : (side + 1) * 256]
            swapped = jnp.concatenate([values[:, 128:], values[:, :128]], axis=1)
            spread.append((real_mask * values).astype(BF16))
            spread.append((imag_mask * swapped).astype(BF16))
        lanes = slice(group * 256, (group + 1) * 256)
        cross = lax.dot_general(
            jnp.concatenate(spread, axis=0),
            jnp.concatenate([own_ref[:, lanes], sibling_ref[:, lanes]], axis=0),
            (((1,), (1,)), ((), ())),
            preferred_element_type=F32,
        ).astype(BF16)
        rows = slice(group * 32, (group + 1) * 32)
        for slot in range(SLOTS):
            cross_ref[rows, slot * 128 : (slot + 1) * 128] = cross[slot * 32 : (slot + 1) * 32]

    for line_row in range(16):
        for side in range(2):
            group_step(line_row, side)
    for side in range(2):
        lanes = slice(side * 1024, (side + 1) * 1024)
        result = jnp.dot(
            lag_ref[...], cross_ref[:, lanes], preferred_element_type=F32
        ).astype(BF16)
        for block in range(8):
            for part in range(4):
                out_ref[part, block, :, side * 128 : (side + 1) * 128] = result[
                    part * 64 : (part + 1) * 64, block * 128 : (block + 1) * 128
                ]


def spread_kernel(in_ref, out_hbm, wide_ref, sems):
    sends = []
    for far_side in range(2):
        for core in range(2):
            for far in range(2):
                for pair in range(2):
                    left = in_ref[far_side, core, far, 2 * pair].astype(F32)
                    right = in_ref[far_side, core, far, 2 * pair + 1].astype(F32)
                    for part in range(4):
                        side, half = part // 2, part % 2
                        lanes = slice(part * LINE, (part + 1) * LINE)
                        spot = far_side * 1024 + (core ^ half) * 512 + far * 256 + pair * 128
                        wide_ref[2 * core + side, :, spot : spot + 128] = jnp.concatenate(
                            [left[:, lanes], right[:, lanes]], axis=1
                        )
            for side in range(2):
                spot = pl.ds(far_side * 1024, 1024)
                send = pltpu.make_async_copy(
                    wide_ref.at[2 * core + side, :, spot],
                    out_hbm.at[2 * core + side, :, spot],
                    sems.at[len(sends)],
                )
                send.start()
                sends.append(send)
    for send in sends:
        send.wait()


def vmem():
    return pl.BlockSpec(memory_space=pltpu.VMEM)


def smem():
    return pl.BlockSpec(memory_space=pltpu.SMEM)


def whole():
    return pl.BlockSpec(memory_space=pl.ANY)


SMALL = pltpu.CompilerParams(vmem_limit_bytes=12 * 1024 * 1024)
MEDIUM = pltpu.CompilerParams(vmem_limit_bytes=20 * 1024 * 1024)
FULL = pltpu.CompilerParams(vmem_limit_bytes=60 * 1024 * 1024)


def call_whiten(base, records, dead_list):
    return pl.pallas_call(
        whiten_kernel,
        out_shape=jax.ShapeDtypeStruct((OWN, WIDE), BF16),
        in_specs=[smem(), whole(), whole(), whole(), whole(), whole(), vmem()],
        out_specs=whole(),
        scratch_shapes=[
            pltpu.VMEM((OWN, 32768), F32),
            pltpu.VMEM((512, 256), BF16),
            pltpu.VMEM((2, 3, NT // 4, NBINS // 2), BF16),
            pltpu.VMEM((3, NT // 2, NBINS), BF16),
            pltpu.VMEM((NBINS, NBINS), BF16),
            pltpu.VMEM((SEG * OWN, NT), F32),
            pltpu.VMEM((OWN, WIDE), BF16),
            pltpu.SemaphoreType.DMA((12,)),
        ],
        compiler_params=FULL,
        name="whiten",
    )(
        base,
        records,
        jnp.asarray(fir_table()),
        jnp.asarray(even_table()),
        jnp.asarray(odd_table()),
        jnp.asarray(smooth_table()),
        dead_list.reshape(1, 32),
    )


def call_pick(place, sources, parts):
    return pl.pallas_call(
        pick_kernel,
        out_shape=(
            jax.ShapeDtypeStruct((PLANE, 2 * SEG, NBINS), BF16),
            jax.ShapeDtypeStruct((LINE, WIDE), BF16),
        ),
        in_specs=[smem(), smem()] + [vmem()] * 5,
        out_specs=(vmem(), vmem()),
        scratch_shapes=[pltpu.VMEM((4, 17 * LINE, 128), F32)],
        compiler_params=SMALL,
        name="pick",
    )(place, sources, *parts)


def call_keep(part):
    return pl.pallas_call(
        keep_kernel,
        out_shape=jax.ShapeDtypeStruct((OWN, WIDE), BF16),
        in_specs=[vmem()],
        out_specs=vmem(),
        compiler_params=SMALL,
        cost_estimate=pl.CostEstimate(flops=0, bytes_accessed=1048576, transcendentals=0),
        name="keep",
    )(part)


def call_hold(slot, sources, arrived):
    return pl.pallas_call(
        hold_kernel,
        out_shape=jax.ShapeDtypeStruct((SLOTS, 2 * SEG, NBINS), BF16),
        in_specs=[smem(), smem(), vmem()],
        out_specs=vmem(),
        compiler_params=SMALL,
        name="hold",
    )(slot, sources, arrived)


def call_corr(source_spectra, own, sibling):
    return pl.pallas_call(
        corr_kernel,
        out_shape=jax.ShapeDtypeStruct((4, 8, LAGS // 4, 4 * LINE), BF16),
        in_specs=[vmem(), vmem(), vmem(), vmem()],
        out_specs=vmem(),
        scratch_shapes=[
            pltpu.VMEM((SLOTS, 16, 512), F32),
            pltpu.VMEM((2 * NBINS, SLOTS * 2 * LINE), BF16),
        ],
        compiler_params=MEDIUM,
        name="correlate",
    )(source_spectra, own, sibling, jnp.asarray(lag_table()))


def call_spread(gathered):
    return pl.pallas_call(
        spread_kernel,
        out_shape=jax.ShapeDtypeStruct((4, LAGS // 4, PLANE * LINE), F32),
        in_specs=[vmem()],
        out_specs=whole(),
        scratch_shapes=[
            pltpu.VMEM((4, LAGS // 4, PLANE * LINE), F32),
            pltpu.SemaphoreType.DMA((8,)),
        ],
        compiler_params=SMALL,
        name="spread",
    )(gathered)


def shards(records, sources, dead_list):
    xl_pos = lax.axis_index("xl")
    core_pos = lax.axis_index("core")
    xh_pos = lax.axis_index("xh")
    z_pos = lax.axis_index("z")
    y_pos = lax.axis_index("y")
    chan_pos = (xh_pos * 4 + z_pos) * 4 + y_pos
    device = (xl_pos * 2 + core_pos) * 32 + chan_pos
    own_slot = 4 * chan_pos + core_pos * 2 + xl_pos
    whitened = call_whiten((device * OWN).reshape(1), records, dead_list)
    up = [(i, (i + 1) % GROUP) for i in range(GROUP)]
    down = [(i, (i - 1) % GROUP) for i in range(GROUP)]
    after = lax.ppermute(whitened, "y", down)
    before = lax.ppermute(whitened, "y", up)
    kept = call_keep(whitened)
    kept, after, before = lax.optimization_barrier((kept, after, before))
    left = lax.ppermute(after[:, : WIDE // 2], "y", down)
    right = lax.ppermute(before[:, WIDE // 2 :], "y", up)
    parts = [kept, after, left, right, before]
    picked, line = call_pick(y_pos.reshape(1), sources, parts)
    arrived = lax.all_to_all(picked, PLANE_AXES, 0, 0, tiled=True)
    arrived, sent_line = lax.optimization_barrier((arrived, line))
    sibling_line = lax.ppermute(sent_line, "core", [(0, 1), (1, 0)])
    held = call_hold(own_slot.reshape(1), sources, arrived)
    source_spectra = lax.all_to_all(held, SIDE_AXES, 0, 0, tiled=True)
    blocks = call_corr(source_spectra, sent_line, sibling_line)
    gathered = lax.all_to_all(
        blocks.reshape(PLANE, LAGS // 4, 4 * LINE), PLANE_AXES, 0, 0, tiled=True
    )
    return call_spread(gathered.reshape(2, 2, 2, 4, LAGS // 4, 4 * LINE))


def solution(mesh):
    inner = Mesh(mesh.devices.reshape(2, 2, 2, 4, 4), AXES)
    return jax.shard_map(
        shards,
        mesh=inner,
        in_specs=(P(AXES, None), P(), P()),
        out_specs=P(("xh", "z", "y"), ("xl", "core"), None),
        check_vma=False,
    )
```
